256 devices in a mesh: seq: 32 (over x, z_hi, core), head: 8 (over z_lo, y).
Axes of the slice: x: 4, y: 4, z: 8 (z_hi: 4, z_lo: 2; z = z_hi * 2 + z_lo), core: 2. Of those that a mesh axis runs over, the one named last changes fastest.
Arguments:
- queries: bfloat16 [4096, 24576], P('seq', 'head'), may hold values from -200 to 200
- latent_keys: bfloat16 [4096, 576], P('seq'), may hold values from -8 to 8
- w_key_up: bfloat16 [128, 128, 512], P('head'), may hold values from -0.5 to 0.5
- w_value_up: bfloat16 [128, 512, 128], P('head'), may hold values from -0.25 to 0.25
- slab_order: int32 [32], replicated, may hold values from 0 to 31, each once
- segment_ids: int32 [4096], replicated, may hold values from 0 to 1, as said below
Outputs:
- attended: bfloat16 [4096, 16384], P(('seq', 'head'))
The draws below stay inside these ranges and needn't reach their ends.
Inputs may be any that keep to these rules, and one draw needn't show every extreme that they name: `slab_order`: a permutation of the slab indices. `segment_ids`: never falls along positions; starts at 0, ends at 1, and each of the two transcripts holds 1024 positions or more.
All inputs are finite; a program needn't handle non-finite values.
Results may differ from the reference program's by a relative error of at most 0.0075.
Values may be sent and summed in bfloat16 or wider, within the bound.
A program may use at most 64 MiB of HBM per device.

```python
import jax
import jax.numpy as jnp
from jax import lax

HEADS = 128
NOPE = 128
ROPE = 64
LATENT = 512
VHEAD = 128
TOKENS = 4096
N_SEQ = 32


def draw_queries(key, part):
    key = jax.random.fold_in(key, 11)
    first, second = jax.random.split(key, 2)
    nope_part = jnp.clip(jax.random.normal(first, (TOKENS, HEADS, NOPE), jnp.float32), -6.0, 6.0)
    rope_part = jnp.clip(jax.random.normal(second, (TOKENS, HEADS, ROPE), jnp.float32), -6.0, 6.0)
    joined = jnp.concatenate([nope_part, rope_part], axis=2)
    return joined.reshape(TOKENS, HEADS * (NOPE + ROPE)).astype(jnp.bfloat16)


def draw_latent_keys(key, part):
    key = jax.random.fold_in(key, 23)
    first, second = jax.random.split(key, 2)
    latent = jnp.clip(jax.random.normal(first, (TOKENS, LATENT), jnp.float32), -6.0, 6.0)
    rotary = jnp.clip(jax.random.normal(second, (TOKENS, ROPE), jnp.float32), -6.0, 6.0)
    return jnp.concatenate([latent, rotary], axis=1).astype(jnp.bfloat16)


def draw_segment_ids(key, part):
    key = jax.random.fold_in(key, 37)
    boundary = jax.random.randint(key, (), TOKENS // 4, TOKENS - TOKENS // 4 + 1, dtype=jnp.int32)
    positions = jnp.arange(TOKENS, dtype=jnp.int32)
    return (positions >= boundary).astype(jnp.int32)


def level_of(stream_key, dims, cuts, smallest, top_value):
    def one(dim, shards_of):
        draws = jax.random.uniform(jax.random.fold_in(jax.random.fold_in(stream_key, 6), dim), (shards_of,), jnp.float32, smallest / len(cuts), top_value / len(cuts))
        return jnp.repeat(jnp.exp(draws), dims[dim] // shards_of).reshape((-1,) + (1,) * (len(dims) - dim - 1))

    gain = one(*cuts[0])
    for cut in cuts[1:]:
        gain = gain * one(*cut)
    return gain


def centred(key, shape, width, limit, pieces=(), held_as=jnp.bfloat16):
    values = width * jax.random.normal(key, shape, jnp.float32)
    if pieces:
        values = values * level_of(key, shape, pieces, -0.22, 0.18)
    return jnp.clip(values, -limit, limit).astype(held_as)


def setup_inputs(seed: int = 0) -> dict:
    arg_keys = jax.random.split(jax.random.key(seed), 7)
    return {
        "queries": draw_queries(jax.random.fold_in(arg_keys[6], 71), 0),
        "latent_keys": draw_latent_keys(jax.random.fold_in(arg_keys[6], 71), 0),
        "w_key_up": centred(arg_keys[2], (HEADS, NOPE, LATENT), NOPE ** -0.5, 0.5, ((0, 8),)),
        "w_value_up": centred(arg_keys[3], (HEADS, LATENT, VHEAD), LATENT ** -0.5, 0.25, ((0, 8),)),
        "slab_order": jax.random.permutation(arg_keys[4], N_SEQ).astype(jnp.int32),
        "segment_ids": draw_segment_ids(jax.random.fold_in(arg_keys[6], 71), 0),
    }


negative_fill = -1.0e30


def reference(queries, latent_keys, w_key_up, w_value_up, slab_order, segment_ids):
    total_rows = queries.shape[0]
    slab_rows = total_rows // N_SEQ
    stored = jnp.arange(total_rows, dtype=jnp.int32)
    position = slab_order[stored // slab_rows] * slab_rows + stored % slab_rows
    transcript = segment_ids[position]
    live = (position[None, :] <= position[:, None]) & (transcript[None, :] == transcript[:, None])
    shaped = queries.reshape(total_rows, HEADS, NOPE + ROPE)
    latent = latent_keys[:, :LATENT]
    key_rope = latent_keys[:, LATENT:]
    scale = (NOPE + ROPE) ** -0.5

    def one_head(packed):
        head_query, key_up, value_up = packed
        absorbed = jnp.dot(head_query[:, :NOPE], key_up, preferred_element_type=jnp.float32).astype(jnp.bfloat16)
        scores = jnp.dot(absorbed, latent.T, preferred_element_type=jnp.float32)
        scores = scores + jnp.dot(head_query[:, NOPE:], key_rope.T, preferred_element_type=jnp.float32)
        scores = scores * scale
        masked = jnp.where(live, scores, negative_fill)
        top = jnp.max(masked, axis=1, keepdims=True)
        weights = jnp.where(live, jnp.exp(masked - top), 0.0)
        summed = jnp.sum(weights, axis=1, keepdims=True)
        context = (jnp.dot(weights.astype(jnp.bfloat16), latent, preferred_element_type=jnp.float32) / summed).astype(jnp.bfloat16)
        return jnp.dot(context, value_up, preferred_element_type=jnp.float32).astype(jnp.bfloat16)

    outputs = lax.map(one_head, (shaped.transpose(1, 0, 2), w_key_up, w_value_up))
    return outputs.transpose(1, 0, 2).reshape(total_rows, HEADS * VHEAD)
```

```python
import functools

import jax
import jax.numpy as jnp
from jax import lax
from jax.experimental import pallas as pl
from jax.experimental.pallas import tpu as pltpu
from jax.sharding import PartitionSpec as P

MESH = pl.DeviceIdType.MESH
BF16 = jnp.bfloat16
F32 = jnp.float32

HEADS = 16
ROWS = 128
NOPE, ROPE, LATENT, VHEAD = 128, 64, 512, 128
KEY = LATENT + ROPE
WIDE = KEY + ROWS
SLABS = 32
WINDOW = 24
PAIR = 2 * ROWS
STEPS = HEADS // 2
CHUNK = 512
NEGATIVE = -1.0e30
LOG2E = 1.4426950408889634


def dot(a, b):
    return jnp.dot(a, b, preferred_element_type=F32)


def kernel(
    order, segment, latent, queries_hbm, w_key_hbm, w_value_hbm, out,
    gathered, wide_q, key_t, value, scores, tops, attended, queries, w_key, w_value,
    listed, load_sem, send_sem, recv_sem, half_sem, out_send, out_recv,
):
    seq, head = lax.axis_index("seq"), lax.axis_index("head")
    core, zh, x = seq % 2, (seq // 2) % 4, seq // 8
    y, zl = head % 4, head // 4

    def slab(x_of, zh_of, core_of):
        return (x_of * 4 + zh_of) * 2 + core_of

    x_up, x_down, x_far = (x + 1) % 4, (x + 3) % 4, (x + 2) % 4
    zh_outer = (zh + 3 + 2 * zl) % 4
    zh_inner = (zh + 5 - 2 * zl) % 4
    zh_far = (zh + 2) % 4
    up = (slab(x_up, zh, core), head)
    down = (slab(x_down, zh, core), head)
    outer = (slab(x, zh_outer, core), (1 - zl) * 4 + y)
    inner = (seq, (1 - zl) * 4 + y)
    twin = (slab(x, zh, 1 - core), head)
    mates = [(seq, (head + 1 + i) % 8) for i in range(7)]

    loads = [
        pltpu.make_async_copy(queries_hbm, queries, load_sem.at[0]),
        pltpu.make_async_copy(w_key_hbm, w_key, load_sem.at[1]),
        pltpu.make_async_copy(w_value_hbm, w_value, load_sem.at[2]),
    ]
    for load in loads:
        load.start()
    gathered[seq] = latent[...]

    barrier = pltpu.get_barrier_semaphore()
    greeted = [up, down, outer, twin] + mates
    for device in greeted:
        pl.semaphore_signal(barrier, inc=1, device_id=device, device_id_type=MESH)
    pl.semaphore_wait(barrier, len(greeted))

    def piece(index, half):
        if half is None:
            return gathered.at[index]
        return gathered.at[index, pl.ds(pl.multiple_of(half * 64, 64), 64)]

    def transfer(index, device, sent, half=None):
        arrived = recv_sem.at[index] if half is None else half_sem.at[half]
        return pltpu.make_async_remote_copy(
            src_ref=piece(index, half), dst_ref=piece(index, half),
            send_sem=send_sem.at[sent], recv_sem=arrived,
            device_id=device, device_id_type=MESH,
        )

    sent = ([], [])

    def send(which, index, device, half=None):
        transfer(index, device, len(sent[which]), half).start()
        sent[which].append(half)

    def arrive(index, half=None):
        transfer(index, twin, 0, half).wait_recv()

    @pl.when(core == 0)
    def _():
        for device in (up, down, twin, outer):
            send(0, seq, device)

    @pl.when(core == 1)
    def _():
        for device in (outer, twin, up, down):
            send(1, seq, device)

    def search(_, span):
        low, high = span
        middle = (low + high) // 2
        first = segment[middle] == 0
        return jnp.where(first, middle + 1, low), jnp.where(first, high, middle)

    boundary, _ = lax.fori_loop(0, 12, search, (0, SLABS * ROWS - 1))
    my_slab = order[seq]

    def invert(step, _):
        wanted = jnp.maximum(my_slab - step, 0)
        found = 0
        for b in range(1, SLABS):
            found = jnp.where(order[b] == wanted, b, found)
        listed[step] = found
        return 0

    lax.fori_loop(0, WINDOW, invert, 0)

    loads[0].wait()
    loads[1].wait()
    row = lax.broadcasted_iota(jnp.int32, (ROWS, ROWS), 0)
    column = lax.broadcasted_iota(jnp.int32, (ROWS, ROWS), 1)
    one_hot = (row == column).astype(BF16)

    def absorb(j, _):
        two = queries[:, pl.ds(pl.multiple_of(j * 384, 384), 384)]
        for i in range(2):
            mine = two[:, i * 192 : i * 192 + 192]
            rows = pl.ds(pl.multiple_of((2 * j + i) * ROWS, ROWS), ROWS)
            wide_q[rows, :LATENT] = dot(mine[:, :NOPE], w_key[2 * j + i]).astype(BF16)
            wide_q[rows, LATENT:] = jnp.concatenate([mine[:, NOPE:], one_hot], axis=1)
        return 0

    lax.fori_loop(0, HEADS // 2, absorb, 0)

    @pl.when(core == 0)
    def _():
        def mine(x_of, zh_of):
            return slab(x_of, zh_of, 0)

        def turned(k):
            return (x + k) % 4

        arrive(mine(x_down, zh))
        send(0, mine(x_down, zh), up, 0)
        send(0, mine(x_down, zh), outer)
        send(0, mine(x_down, zh), twin)
        arrive(mine(x_up, zh))
        send(0, mine(x_up, zh), down, 1)
        send(0, mine(x_up, zh), outer)
        send(0, mine(x_up, zh), twin)
        arrive(mine(x_far, zh), 0)
        arrive(mine(x_far, zh), 1)
        send(0, mine(x_far, zh), outer)
        send(0, mine(x_far, zh), twin)
        for k in (0, 3, 1, 2):
            arrive(mine(turned(k), zh_outer))
            send(0, mine(turned(k), zh_outer), inner)
            send(0, mine(turned(k), zh_outer), twin)
        for k in (zl, 3 - zl):
            arrive(mine(turned(k), zh_inner))
            send(0, mine(turned(k), zh_inner), outer)
            send(0, mine(turned(k), zh_inner), twin)
        for k in (1 - zl, 2 + zl):
            arrive(mine(turned(k), zh_inner))
            send(0, mine(turned(k), zh_inner), twin)
        for k in (1 - zl, 2 + zl):
            arrive(mine(turned(k), zh_far))
            send(0, mine(turned(k), zh_far), inner)
            send(0, mine(turned(k), zh_far), twin)
        for k in (zl, 3 - zl):
            arrive(mine(turned(k), zh_far))
            send(0, mine(turned(k), zh_far), twin)
        for x_of in range(4):
            for zh_of in range(4):
                arrive(slab(x_of, zh_of, 1))

    @pl.when(core == 1)
    def _():
        def mine(x_of, zh_of):
            return slab(x_of, zh_of, 1)

        arrive(mine(x, zh_outer))
        send(1, mine(x, zh_outer), inner)
        for device in (up, down, twin):
            send(1, mine(x, zh_outer), device)
        arrive(mine(x, zh_inner))
        send(1, mine(x, zh_inner), outer, zl)
        for device in (up, down, twin):
            send(1, mine(x, zh_inner), device)
        arrive(mine(x, zh_far), 1 - zl)
        send(1, mine(x, zh_far), inner, 1 - zl)
        arrive(mine(x, zh_far), zl)
        for device in (up, down, twin):
            send(1, mine(x, zh_far), device)
        for j, zh_of in enumerate((zh, zh_outer, zh_inner, zh_far)):
            arrive(mine(x_down, zh_of))
            if j < 2:
                send(1, mine(x_down, zh_of), up)
            send(1, mine(x_down, zh_of), twin)
            arrive(mine(x_up, zh_of))
            if j >= 2:
                send(1, mine(x_up, zh_of), down)
            send(1, mine(x_up, zh_of), twin)
        for zh_of in (zh, zh_outer, zh_inner, zh_far):
            arrive(mine(x_far, zh_of))
            send(1, mine(x_far, zh_of), twin)
        for x_of in range(4):
            for zh_of in range(4):
                arrive(slab(x_of, zh_of, 0))

    query_pos = my_slab * ROWS + row
    first_live = jnp.where(query_pos >= boundary, boundary, 0)

    def take(step, _):
        held = gathered[listed[step]]
        here = pl.ds(pl.multiple_of(step * ROWS, ROWS), ROWS)
        value[here, :] = held[:, :LATENT]
        key_t[:KEY, here] = held.T
        key_pos = (my_slab - step) * ROWS + column
        live = (key_pos >= first_live) & (key_pos <= query_pos)
        key_t[KEY:, here] = jnp.where(live, 0.0, NEGATIVE).astype(BF16)
        return 0

    lax.fori_loop(0, WINDOW, take, 0)
    loads[2].wait()

    scale = (NOPE + ROPE) ** -0.5 * LOG2E
    chunks = [pl.ds(i * CHUNK, CHUNK) for i in range(WINDOW * ROWS // CHUNK)]

    def score(q, chunk, slot, top):
        s = dot(q, key_t[:, chunk])
        scores[slot, :, chunk] = s
        for i in range(0, CHUNK, 128):
            part = s[:, i : i + 128]
            top = part if top is None else jnp.maximum(top, part)
        return top

    def q_rows(step):
        return wide_q[pl.ds(pl.multiple_of(step * PAIR, PAIR), PAIR), :]

    def attend(step, slot, ahead):
        top = jnp.max(tops[slot], axis=1, keepdims=True) * scale
        context, total, next_top = jnp.zeros((PAIR, LATENT), F32), jnp.zeros((PAIR, 128), F32), None
        for chunk in chunks:
            if ahead:
                next_top = score(q_rows(step + 1), chunk, 1 - slot, next_top)
            weights = jnp.exp2(scores[slot, :, chunk] * scale - top)
            for i in range(0, CHUNK, 128):
                total = total + weights[:, i : i + 128]
            context = context + dot(weights.astype(BF16), value[chunk, :])
        if ahead:
            tops[1 - slot] = next_top
        context = (context / jnp.sum(total, axis=1, keepdims=True)).astype(BF16)
        for i in range(2):
            h = 2 * step + i
            attended[:, pl.ds(pl.multiple_of(h * VHEAD, VHEAD), VHEAD)] = dot(
                context[i * ROWS : (i + 1) * ROWS], w_value[h]
            ).astype(BF16)
        for i in range(7):
            deliver(step, i).start()

    def columns_of(who, step):
        return pl.ds(pl.multiple_of(who * (HEADS * VHEAD) + step * PAIR, PAIR), PAIR)

    def deliver(step, i):
        mate = mates[i][1]
        return pltpu.make_async_remote_copy(
            src_ref=attended.at[pl.ds(pl.multiple_of(mate * 16, 16), 16), columns_of(0, step)],
            dst_ref=out.at[:, columns_of(head, step)],
            send_sem=out_send.at[step, i], recv_sem=out_recv.at[step, i],
            device_id=mates[i], device_id_type=MESH,
        )

    top = None
    for chunk in chunks:
        top = score(q_rows(0), chunk, 0, top)
    tops[0] = top

    def two_steps(i, _):
        attend(2 * i, 0, True)
        attend(2 * i + 1, 1, True)
        return 0

    lax.fori_loop(0, STEPS // 2 - 1, two_steps, 0)
    attend(STEPS - 2, 0, True)
    attend(STEPS - 1, 1, False)

    out[:, pl.ds(pl.multiple_of(head * (HEADS * VHEAD), 128), HEADS * VHEAD)] = attended[
        pl.ds(pl.multiple_of(head * 16, 16), 16), :
    ]

    for which in range(2):

        @pl.when(core == which)
        def _(which=which):
            for number, half in enumerate(sent[which]):
                transfer(seq, twin, number, None if half is None else 0).wait_send()

    def finish(step, _):
        for i in range(7):
            deliver(step, i).wait_send()
            sender = (head + 7 - i) % 8
            pltpu.make_async_remote_copy(
                src_ref=attended.at[pl.ds(0, 16), columns_of(0, step)],
                dst_ref=out.at[:, columns_of(sender, step)],
                send_sem=out_send.at[step, i], recv_sem=out_recv.at[step, i],
                device_id=mates[i], device_id_type=MESH,
            ).wait_recv()
        return 0

    lax.fori_loop(0, STEPS, finish, 0)


def shards(queries, latent_keys, w_key_up, w_value_up, slab_order, segment_ids):
    keys = WINDOW * ROWS
    return pl.pallas_call(
        kernel,
        out_shape=jax.ShapeDtypeStruct((16, 8 * HEADS * VHEAD), BF16),
        in_specs=[
            pl.BlockSpec(memory_space=pltpu.SMEM),
            pl.BlockSpec(memory_space=pltpu.SMEM),
            pl.BlockSpec(memory_space=pltpu.VMEM),
            pl.BlockSpec(memory_space=pl.ANY),
            pl.BlockSpec(memory_space=pl.ANY),
            pl.BlockSpec(memory_space=pl.ANY),
        ],
        out_specs=pl.BlockSpec(memory_space=pltpu.VMEM),
        scratch_shapes=[
            pltpu.VMEM((SLABS, ROWS, KEY), BF16),
            pltpu.VMEM((HEADS * ROWS, WIDE), BF16),
            pltpu.VMEM((WIDE, keys), BF16),
            pltpu.VMEM((keys, LATENT), BF16),
            pltpu.VMEM((2, PAIR, keys), F32),
            pltpu.VMEM((2, PAIR, 128), F32),
            pltpu.VMEM((ROWS, HEADS * VHEAD), BF16),
            pltpu.VMEM((ROWS, HEADS * (NOPE + ROPE)), BF16),
            pltpu.VMEM((HEADS, NOPE, LATENT), BF16),
            pltpu.VMEM((HEADS, LATENT, VHEAD), BF16),
            pltpu.SMEM((WINDOW,), jnp.int32),
            pltpu.SemaphoreType.DMA((3,)),
            pltpu.SemaphoreType.DMA((32,)),
            pltpu.SemaphoreType.DMA((SLABS,)),
            pltpu.SemaphoreType.DMA((2,)),
            pltpu.SemaphoreType.DMA((STEPS, 7)),
            pltpu.SemaphoreType.DMA((STEPS, 7)),
        ],
        compiler_params=pltpu.CompilerParams(
            collective_id=0, has_side_effects=True, vmem_limit_bytes=56 * 2**20
        ),
        cost_estimate=pl.CostEstimate(
            flops=16 * 10**9, bytes_accessed=6 * 2**20, transcendentals=6 * 10**6
        ),
    )(slab_order, segment_ids, latent_keys, queries, w_key_up, w_value_up)


def solution(mesh):
    in_specs = (
        P("seq", "head"),
        P("seq", None),
        P("head", None, None),
        P("head", None, None),
        P(),
        P(),
    )
    out_specs = P(("seq", "head"), None)
    return jax.shard_map(shards, mesh=mesh, in_specs=in_specs, out_specs=out_specs, check_vma=False)
```

```python
import functools

import jax
import jax.numpy as jnp
from jax import lax
from jax.experimental import pallas as pl
from jax.experimental.pallas import tpu as pltpu
from jax.sharding import PartitionSpec as P

MESH = pl.DeviceIdType.MESH
BF16 = jnp.bfloat16
F32 = jnp.float32

HEADS = 16
ROWS = 128
NOPE, ROPE, LATENT, VHEAD = 128, 64, 512, 128
KEY = LATENT + ROPE
HALF = KEY // 2
WIDE = KEY + ROWS
SLABS = 32
BAND = 8
PAIR = 2 * ROWS
STEPS = HEADS // 2
CHUNK = 256
NEGATIVE = -1.0e30
LOG2E = 1.4426950408889634


def dot(a, b):
    return jnp.dot(a, b, preferred_element_type=F32)


def kernel(
    order, segment, latent, queries_hbm, w_key_hbm, w_value_hbm, out,
    own_band, outer_band, inner_band, far_band, wide_q, value, scores, tops, best, total, context,
    attended, queries, w_key, w_value, load_sem, send_sem, recv_sem, out_send, out_recv,
):
    seq, head = lax.axis_index("seq"), lax.axis_index("head")
    core, zh, x = seq % 2, (seq // 2) % 4, seq // 8
    y, zl = head % 4, head // 4

    def slab(x_of, zh_of, core_of):
        return (x_of * 4 + zh_of) * 2 + core_of

    x_up, x_down, x_far = (x + 1) % 4, (x + 3) % 4, (x + 2) % 4
    zh_outer = (zh + 3 + 2 * zl) % 4
    zh_inner = (zh + 5 - 2 * zl) % 4
    zh_far = (zh + 2) % 4
    up = (slab(x_up, zh, core), head)
    down = (slab(x_down, zh, core), head)
    outer = (slab(x, zh_outer, core), (1 - zl) * 4 + y)
    inner = (seq, (1 - zl) * 4 + y)
    twin = (slab(x, zh, 1 - core), head)
    y_up = (seq, zl * 4 + (y + 1) % 4)
    y_down = (seq, zl * 4 + (y + 3) % 4)
    mates = [(seq, (head + 1 + i) % 8) for i in range(7)]

    loads = [
        pltpu.make_async_copy(queries_hbm, queries, load_sem.at[0]),
        pltpu.make_async_copy(w_key_hbm, w_key, load_sem.at[1]),
        pltpu.make_async_copy(w_value_hbm, w_value, load_sem.at[2]),
    ]
    for load in loads:
        load.start()
    bands = (own_band, outer_band, inner_band, far_band)
    own_band[x * 2 + core, :KEY] = latent[...]

    barrier = pltpu.get_barrier_semaphore()
    greeted = [up, down, outer, twin] + mates
    for device in greeted:
        pl.semaphore_signal(barrier, inc=1, device_id=device, device_id_type=MESH)
    pl.semaphore_wait(barrier, len(greeted))

    def transfer(band, landing, k, half, device, sent, core_of):
        place = ((x + k) % 4) * 2 + core_of
        span = pl.ds(pl.multiple_of(half * HALF, 16), HALF)
        return pltpu.make_async_remote_copy(
            src_ref=bands[band].at[place, span], dst_ref=bands[landing].at[place, span],
            send_sem=send_sem.at[sent], recv_sem=recv_sem.at[landing, place, half],
            device_id=device, device_id_type=MESH,
        )

    sent = []

    def send(band, landing, k, half, *devices):
        for device in devices:
            transfer(band, landing, k, half, device, len(sent), core).start()
            sent.append(device)

    def arrive(band, k, half, core_of=core):
        transfer(band, band, k, half, twin, 0, core_of).wait_recv()

    kept, other = y % 2, 1 - y % 2
    for half in range(2):
        send(0, 0, 0, half, up, down)
    send(0, 1, 0, kept, outer)
    for half in range(2):
        send(0, 0, 0, half, twin)

    def search(_, span):
        low, high = span
        middle = (low + high) // 2
        first = segment[middle] == 0
        return jnp.where(first, middle + 1, low), jnp.where(first, high, middle)

    boundary, _ = lax.fori_loop(0, 12, search, (0, SLABS * ROWS - 1))
    my_slab = order[seq]

    loads[0].wait()
    loads[1].wait()
    row = lax.broadcasted_iota(jnp.int32, (ROWS, ROWS), 0)
    column = lax.broadcasted_iota(jnp.int32, (ROWS, ROWS), 1)
    one_hot = (row == column).astype(BF16)

    def absorb(j, _):
        two = queries[:, pl.ds(pl.multiple_of(j * 384, 384), 384)]
        for i in range(2):
            mine = two[:, i * 192 : i * 192 + 192]
            rows = pl.ds(pl.multiple_of((2 * j + i) * ROWS, ROWS), ROWS)
            wide_q[rows, :LATENT] = dot(mine[:, :NOPE], w_key[2 * j + i]).astype(BF16)
            wide_q[rows, LATENT:] = jnp.concatenate([mine[:, NOPE:], one_hot], axis=1)
        return 0

    lax.fori_loop(0, HEADS // 2, absorb, 0)

    query_pos = my_slab * ROWS + row
    first_live = jnp.where(query_pos >= boundary, boundary, 0)

    def cover(place, _):
        for band, zh_of in enumerate((zh, zh_outer, zh_inner, zh_far)):
            key_pos = order[slab(place // 2, zh_of, place % 2)] * ROWS + column
            live = (key_pos >= first_live) & (key_pos <= query_pos)
            bands[band][place, KEY:] = jnp.where(live, 0.0, NEGATIVE).astype(BF16)
        return 0

    lax.fori_loop(0, BAND, cover, 0)

    sideways = {0: y_up, 3: y_up, 1: y_down, 2: y_down}

    def along_x(k, onward, passed):
        arrive(0, k, 0)
        arrive(0, k, 1)
        if onward is not None:
            send(0, 0, k, passed, onward)
        send(0, 1, k, kept, outer)
        for half in range(2):
            send(0, 0, k, half, twin)

    def from_outer(k):
        arrive(1, k, kept)
        send(1, 2, k, kept, inner)
        send(1, 1, k, kept, sideways[k], twin)

    def from_inner(k):
        arrive(2, k, kept)
        send(2, 2, k, kept, sideways[k], twin)

    def far_outer(k, side):
        arrive(3, k, kept)
        send(3, 3, k, kept, inner, side, twin)

    def far_inner(k, side):
        arrive(3, k, kept)
        send(3, 3, k, kept, side, twin)

    def from_side(band, k):
        arrive(band, k, other)
        send(band, band, k, other, twin)

    def complete(band):
        for k in range(4):
            for half in range(2):
                arrive(band, k, half, 1 - core)

    along_x(3, up, 0)
    along_x(1, down, 1)
    from_outer(0)
    along_x(2, None, None)
    from_inner(0)
    complete(0)

    def during_own(step):
        if step == 0:
            from_outer(3)
        elif step == 1:
            from_outer(1)
            from_outer(2)
        elif step == 2:
            from_inner(3)
            send(2, 3, 3 * zl, kept, outer)
        elif step == 3:
            from_inner(1)
            from_inner(2)
            send(2, 3, 1 + zl, kept, outer)
            from_side(1, 0)
        elif step == 4:
            from_side(1, 3)
            from_side(1, 1)
            from_side(1, 2)
        elif step == 5:
            from_side(2, 0)
        elif step == 6:
            far_outer(3 - 3 * zl, y_up)

    def during_outer(step):
        if step == 0:
            far_outer(2 - zl, y_down)
            from_side(2, 3)
        elif step == 1:
            from_side(2, 1)
            from_side(2, 2)
        elif step == 2:
            far_inner(3 * zl, y_up)
        elif step == 3:
            far_inner(1 + zl, y_down)
        elif step == 4:
            from_side(3, 3 - 3 * zl)
        elif step == 5:
            from_side(3, 2 - zl)
        elif step == 6:
            from_side(3, 3 * zl)

    def during_inner(step):
        if step == 0:
            from_side(3, 1 + zl)

    scale = (NOPE + ROPE) ** -0.5 * LOG2E
    parts = range(0, BAND * ROWS, CHUNK)

    def rows_of(step):
        return pl.ds(pl.multiple_of(step * PAIR, PAIR), PAIR)

    def score(band, q, first, slot, top):
        keys = jnp.concatenate(
            [bands[band][(first + i) // ROWS] for i in range(0, CHUNK, ROWS)], axis=1
        )
        s = dot(q, keys)
        scores[slot, :, pl.ds(first, CHUNK)] = s
        for i in range(0, CHUNK, 128):
            part = s[:, i : i + 128]
            top = part if top is None else jnp.maximum(top, part)
        return top

    def attend(band, step, ahead):
        slot = step % 2
        here = rows_of(step)
        top = jnp.broadcast_to(jnp.max(tops[slot], axis=1, keepdims=True), (PAIR, 128)) * scale
        if band == 0:
            so_far, sums = jnp.zeros((PAIR, LATENT), F32), jnp.zeros((PAIR, 128), F32)
        else:
            before = best[here, :]
            top = jnp.maximum(top, before)
            fade = jnp.exp2(before - top)
            sums = total[here, :] * fade
            so_far = None
        gained, next_top = None, None
        for first in parts:
            if ahead:
                next_top = score(band, wide_q[rows_of(step + 1), :], first, 1 - slot, next_top)
            weights = []
            for i in range(0, CHUNK, 128):
                w = jnp.exp2(scores[slot, :, pl.ds(first + i, 128)] * scale - top)
                sums = sums + w
                weights.append(w.astype(BF16))
            more = dot(jnp.concatenate(weights, axis=1), value[pl.ds(first, CHUNK), :])
            gained = more if gained is None else gained + more
        if ahead:
            tops[1 - slot] = next_top
        if band > 0:
            gained = gained + context[here, :] * jnp.concatenate([fade] * 4, axis=1)
        if band < 3:
            best[here, :] = top
            total[here, :] = sums
            context[here, :] = gained
            return
        finished = (gained / jnp.sum(sums, axis=1, keepdims=True)).astype(BF16)
        for i in range(2):
            h = 2 * step + i
            attended[:, pl.ds(pl.multiple_of(h * VHEAD, VHEAD), VHEAD)] = dot(
                finished[i * ROWS : (i + 1) * ROWS], w_value[h]
            ).astype(BF16)
        for i in range(7):
            deliver(step, i).start()

    def columns_of(who, step):
        return pl.ds(pl.multiple_of(who * (HEADS * VHEAD) + step * PAIR, PAIR), PAIR)

    def deliver(step, i):
        mate = mates[i][1]
        return pltpu.make_async_remote_copy(
            src_ref=attended.at[pl.ds(pl.multiple_of(mate * 16, 16), 16), columns_of(0, step)],
            dst_ref=out.at[:, columns_of(head, step)],
            send_sem=out_send.at[step, i], recv_sem=out_recv.at[step, i],
            device_id=mates[i], device_id_type=MESH,
        )

    for band, between in enumerate((during_own, during_outer, during_inner, None)):
        if band > 0:
            complete(band)
        if band == 3:
            loads[2].wait()

        def turn(place, _, band=band):
            value[pl.ds(pl.multiple_of(place * ROWS, ROWS), ROWS), :] = bands[band][place, :LATENT].T
            return 0

        lax.fori_loop(0, BAND, turn, 0)
        top = None
        for first in parts:
            top = score(band, wide_q[rows_of(0), :], first, 0, top)
        tops[0] = top

        def go(step, _, band=band, between=between):
            attend(band, step, True)
            if between is not None:
                for n in range(STEPS - 1):

                    @pl.when(step == n)
                    def _(n=n):
                        between(n)

            return 0

        lax.fori_loop(0, STEPS - 1, go, 0)
        attend(band, STEPS - 1, False)

    out[:, pl.ds(pl.multiple_of(head * (HEADS * VHEAD), 128), HEADS * VHEAD)] = attended[
        pl.ds(pl.multiple_of(head * 16, 16), 16), :
    ]
    for number in range(len(sent)):
        transfer(0, 0, 0, 0, twin, number, core).wait_send()

    def finish(step, _):
        for i in range(7):
            deliver(step, i).wait_send()
            sender = (head + 7 - i) % 8
            pltpu.make_async_remote_copy(
                src_ref=attended.at[pl.ds(0, 16), columns_of(0, step)],
                dst_ref=out.at[:, columns_of(sender, step)],
                send_sem=out_send.at[step, i], recv_sem=out_recv.at[step, i],
                device_id=mates[i], device_id_type=MESH,
            ).wait_recv()
        return 0

    lax.fori_loop(0, STEPS, finish, 0)


def shards(queries, latent_keys, w_key_up, w_value_up, slab_order, segment_ids):
    rows = HEADS * ROWS
    return pl.pallas_call(
        kernel,
        out_shape=jax.ShapeDtypeStruct((16, 8 * HEADS * VHEAD), BF16),
        in_specs=[
            pl.BlockSpec(memory_space=pltpu.SMEM),
            pl.BlockSpec(memory_space=pltpu.SMEM),
            pl.BlockSpec(memory_space=pltpu.VMEM),
            pl.BlockSpec(memory_space=pl.ANY),
            pl.BlockSpec(memory_space=pl.ANY),
            pl.BlockSpec(memory_space=pl.ANY),
        ],
        out_specs=pl.BlockSpec(memory_space=pltpu.VMEM),
        scratch_shapes=[
            pltpu.VMEM((BAND, WIDE, ROWS), BF16),
            pltpu.VMEM((BAND, WIDE, ROWS), BF16),
            pltpu.VMEM((BAND, WIDE, ROWS), BF16),
            pltpu.VMEM((BAND, WIDE, ROWS), BF16),
            pltpu.VMEM((rows, WIDE), BF16),
            pltpu.VMEM((BAND * ROWS, LATENT), BF16),
            pltpu.VMEM((2, PAIR, BAND * ROWS), F32),
            pltpu.VMEM((2, PAIR, 128), F32),
            pltpu.VMEM((rows, 128), F32),
            pltpu.VMEM((rows, 128), F32),
            pltpu.VMEM((rows, LATENT), F32),
            pltpu.VMEM((ROWS, HEADS * VHEAD), BF16),
            pltpu.VMEM((ROWS, HEADS * (NOPE + ROPE)), BF16),
            pltpu.VMEM((HEADS, NOPE, LATENT), BF16),
            pltpu.VMEM((HEADS, LATENT, VHEAD), BF16),
            pltpu.SemaphoreType.DMA((3,)),
            pltpu.SemaphoreType.DMA((64,)),
            pltpu.SemaphoreType.DMA((4, BAND, 2)),
            pltpu.SemaphoreType.DMA((STEPS, 7)),
            pltpu.SemaphoreType.DMA((STEPS, 7)),
        ],
        compiler_params=pltpu.CompilerParams(
            collective_id=0, has_side_effects=True, vmem_limit_bytes=56 * 2**20
        ),
        cost_estimate=pl.CostEstimate(
            flops=20 * 10**9, bytes_accessed=6 * 2**20, transcendentals=8 * 10**6
        ),
    )(slab_order, segment_ids, latent_keys.T, queries, w_key_up, w_value_up)


def solution(mesh):
    in_specs = (
        P("seq", "head"),
        P("seq", None),
        P("head", None, None),
        P("head", None, None),
        P(),
        P(),
    )
    out_specs = P(("seq", "head"), None)
    return jax.shard_map(shards, mesh=mesh, in_specs=in_specs, out_specs=out_specs, check_vma=False)
```

```python
import functools

import jax
import jax.numpy as jnp
from jax import lax
from jax.experimental import pallas as pl
from jax.experimental.pallas import tpu as pltpu
from jax.sharding import PartitionSpec as P

MESH = pl.DeviceIdType.MESH
BF16 = jnp.bfloat16
F32 = jnp.float32

HEADS = 16
ROWS = 128
NOPE, ROPE, LATENT, VHEAD = 128, 64, 512, 128
KEY = LATENT + ROPE
HALF = KEY // 2
WIDE = KEY + ROWS
SLABS = 32
BAND = 8
PAIR = 2 * ROWS
STEPS = HEADS // 2
CHUNK = 256
NEGATIVE = -1.0e30
LOG2E = 1.4426950408889634


def dot(a, b):
    return jnp.dot(a, b, preferred_element_type=F32)


def kernel(
    order, segment, latent, queries_hbm, w_key_hbm, w_value_hbm, out,
    own_band, outer_band, inner_band, far_band, wide_q, value, scores_0, scores_1, tops_0, tops_1, best, total, context,
    attended, queries, w_key, w_value, load_sem, send_sem, recv_sem, out_send, out_recv,
):
    seq, head = lax.axis_index("seq"), lax.axis_index("head")
    core, zh, x = seq % 2, (seq // 2) % 4, seq // 8
    y, zl = head % 4, head // 4

    def slab(x_of, zh_of, core_of):
        return (x_of * 4 + zh_of) * 2 + core_of

    x_up, x_down, x_far = (x + 1) % 4, (x + 3) % 4, (x + 2) % 4
    zh_outer = (zh + 3 + 2 * zl) % 4
    zh_inner = (zh + 5 - 2 * zl) % 4
    zh_far = (zh + 2) % 4
    up = (slab(x_up, zh, core), head)
    down = (slab(x_down, zh, core), head)
    outer = (slab(x, zh_outer, core), (1 - zl) * 4 + y)
    inner = (seq, (1 - zl) * 4 + y)
    twin = (slab(x, zh, 1 - core), head)
    y_up = (seq, zl * 4 + (y + 1) % 4)
    y_down = (seq, zl * 4 + (y + 3) % 4)
    mates = [(seq, (head + 1 + i) % 8) for i in range(7)]

    loads = [
        pltpu.make_async_copy(queries_hbm, queries, load_sem.at[0]),
        pltpu.make_async_copy(w_key_hbm, w_key, load_sem.at[1]),
        pltpu.make_async_copy(w_value_hbm, w_value, load_sem.at[2]),
    ]
    for load in loads:
        load.start()
    bands = (own_band, outer_band, inner_band, far_band)
    own_band[x * 2 + core, :KEY] = latent[...]

    barrier = pltpu.get_barrier_semaphore()
    greeted = [up, down, outer, twin] + mates
    for device in greeted:
        pl.semaphore_signal(barrier, inc=1, device_id=device, device_id_type=MESH)
    pl.semaphore_wait(barrier, len(greeted))

    def transfer(band, landing, k, half, device, sent, core_of):
        place = ((x + k) % 4) * 2 + core_of
        span = pl.ds(pl.multiple_of(half * HALF, 16), HALF)
        return pltpu.make_async_remote_copy(
            src_ref=bands[band].at[place, span], dst_ref=bands[landing].at[place, span],
            send_sem=send_sem.at[sent], recv_sem=recv_sem.at[landing, place, half],
            device_id=device, device_id_type=MESH,
        )

    sent = []

    def send(band, landing, k, half, *devices):
        for device in devices:
            transfer(band, landing, k, half, device, len(sent), core).start()
            sent.append(device)

    def arrive(band, k, half, core_of=core):
        transfer(band, band, k, half, twin, 0, core_of).wait_recv()

    kept, other = y % 2, 1 - y % 2
    for half in range(2):
        send(0, 0, 0, half, up, down)
    send(0, 1, 0, kept, outer)
    for half in range(2):
        send(0, 0, 0, half, twin)

    def search(_, span):
        low, high = span
        middle = (low + high) // 2
        first = segment[middle] == 0
        return jnp.where(first, middle + 1, low), jnp.where(first, high, middle)

    boundary, _ = lax.fori_loop(0, 12, search, (0, SLABS * ROWS - 1))
    my_slab = order[seq]

    loads[0].wait()
    loads[1].wait()
    row = lax.broadcasted_iota(jnp.int32, (ROWS, ROWS), 0)
    column = lax.broadcasted_iota(jnp.int32, (ROWS, ROWS), 1)
    one_hot = (row == column).astype(BF16)

    def absorb(j, _):
        two = queries[:, pl.ds(pl.multiple_of(j * 384, 384), 384)]
        for i in range(2):
            mine = two[:, i * 192 : i * 192 + 192]
            rows = pl.ds(pl.multiple_of((2 * j + i) * ROWS, ROWS), ROWS)
            wide_q[rows, :LATENT] = dot(mine[:, :NOPE], w_key[2 * j + i]).astype(BF16)
            wide_q[rows, LATENT:] = jnp.concatenate([mine[:, NOPE:], one_hot], axis=1)
        return 0

    lax.fori_loop(0, HEADS // 2, absorb, 0)

    query_pos = my_slab * ROWS + row
    first_live = jnp.where(query_pos >= boundary, boundary, 0)

    def cover(place, _):
        for band, zh_of in enumerate((zh, zh_outer, zh_inner, zh_far)):
            key_pos = order[slab(place // 2, zh_of, place % 2)] * ROWS + column
            live = (key_pos >= first_live) & (key_pos <= query_pos)
            bands[band][place, KEY:] = jnp.where(live, 0.0, NEGATIVE).astype(BF16)
        return 0

    lax.fori_loop(0, BAND, cover, 0)

    sideways = {0: y_up, 3: y_up, 1: y_down, 2: y_down}

    def along_x(k, onward, passed):
        arrive(0, k, 0)
        arrive(0, k, 1)
        if onward is not None:
            send(0, 0, k, passed, onward)
        send(0, 1, k, kept, outer)
        for half in range(2):
            send(0, 0, k, half, twin)

    def from_outer(k):
        arrive(1, k, kept)
        send(1, 2, k, kept, inner)
        send(1, 1, k, kept, sideways[k], twin)

    def from_inner(k):
        arrive(2, k, kept)
        send(2, 2, k, kept, sideways[k], twin)

    def far_outer(k, side):
        arrive(3, k, kept)
        send(3, 3, k, kept, inner, side, twin)

    def far_inner(k, side):
        arrive(3, k, kept)
        send(3, 3, k, kept, side, twin)

    def from_side(band, k):
        arrive(band, k, other)
        send(band, band, k, other, twin)

    def complete(band):
        for k in range(4):
            for half in range(2):
                arrive(band, k, half, 1 - core)

    along_x(3, up, 0)
    along_x(1, down, 1)
    from_outer(0)
    along_x(2, None, None)
    from_inner(0)
    complete(0)

    def during_own(step):
        if step == 0:
            from_outer(3)
        elif step == 1:
            from_outer(1)
            from_outer(2)
        elif step == 2:
            from_inner(3)
            send(2, 3, 3 * zl, kept, outer)
        elif step == 3:
            from_inner(1)
            from_inner(2)
            send(2, 3, 1 + zl, kept, outer)
            from_side(1, 0)
        elif step == 4:
            from_side(1, 3)
            from_side(1, 1)
            from_side(1, 2)
        elif step == 5:
            from_side(2, 0)
        elif step == 6:
            far_outer(3 - 3 * zl, y_up)

    def during_outer(step):
        if step == 0:
            far_outer(2 - zl, y_down)
            from_side(2, 3)
        elif step == 1:
            from_side(2, 1)
            from_side(2, 2)
        elif step == 2:
            far_inner(3 * zl, y_up)
        elif step == 3:
            far_inner(1 + zl, y_down)
        elif step == 4:
            from_side(3, 3 - 3 * zl)
        elif step == 5:
            from_side(3, 2 - zl)
        elif step == 6:
            from_side(3, 3 * zl)

    def during_inner(step):
        if step == 0:
            from_side(3, 1 + zl)

    scale = (NOPE + ROPE) ** -0.5 * LOG2E
    scores, tops = (scores_0, scores_1), (tops_0, tops_1)
    parts = range(0, BAND * ROWS, CHUNK)

    def rows_of(step):
        return pl.ds(pl.multiple_of(step * PAIR, PAIR), PAIR)

    def score(band, q, first, slot, top):
        keys = jnp.concatenate(
            [bands[band][(first + i) // ROWS] for i in range(0, CHUNK, ROWS)], axis=1
        )
        s = dot(q, keys)
        scores[slot][:, pl.ds(first, CHUNK)] = s
        for i in range(0, CHUNK, 128):
            part = s[:, i : i + 128]
            top = part if top is None else jnp.maximum(top, part)
        return top

    def attend(band, step, slot, ahead):
        here = rows_of(step)
        top = jnp.broadcast_to(jnp.max(tops[slot][...], axis=1, keepdims=True), (PAIR, 128)) * scale
        if band == 0:
            so_far, sums = jnp.zeros((PAIR, LATENT), F32), jnp.zeros((PAIR, 128), F32)
        else:
            before = best[here, :]
            top = jnp.maximum(top, before)
            fade = jnp.exp2(before - top)
            sums = total[here, :] * fade
            so_far = None
        gained, next_top = None, None
        for first in parts:
            if ahead:
                next_top = score(band, wide_q[rows_of(step + 1), :], first, 1 - slot, next_top)
            weights = []
            for i in range(0, CHUNK, 128):
                w = jnp.exp2(scores[slot][:, pl.ds(first + i, 128)] * scale - top)
                sums = sums + w
                weights.append(w.astype(BF16))
            more = dot(jnp.concatenate(weights, axis=1), value[pl.ds(first, CHUNK), :])
            gained = more if gained is None else gained + more
        if ahead:
            tops[1 - slot][...] = next_top
        if band > 0:
            gained = gained + context[here, :] * jnp.concatenate([fade] * 4, axis=1)
        if band < 3:
            best[here, :] = top
            total[here, :] = sums
            context[here, :] = gained
            return
        finished = (gained / jnp.sum(sums, axis=1, keepdims=True)).astype(BF16)
        for i in range(2):
            h = 2 * step + i
            attended[:, pl.ds(pl.multiple_of(h * VHEAD, VHEAD), VHEAD)] = dot(
                finished[i * ROWS : (i + 1) * ROWS], w_value[h]
            ).astype(BF16)
        for i in range(7):
            deliver(step, i).start()

    def columns_of(who, step):
        return pl.ds(pl.multiple_of(who * (HEADS * VHEAD) + step * PAIR, PAIR), PAIR)

    def deliver(step, i):
        mate = mates[i][1]
        return pltpu.make_async_remote_copy(
            src_ref=attended.at[pl.ds(pl.multiple_of(mate * 16, 16), 16), columns_of(0, step)],
            dst_ref=out.at[:, columns_of(head, step)],
            send_sem=out_send.at[step, i], recv_sem=out_recv.at[step, i],
            device_id=mates[i], device_id_type=MESH,
        )

    for band, between in enumerate((during_own, during_outer, during_inner, None)):
        if band > 0:
            complete(band)
        if band == 3:
            loads[2].wait()

        def turn(place, _, band=band):
            value[pl.ds(pl.multiple_of(place * ROWS, ROWS), ROWS), :] = bands[band][place, :LATENT].T
            return 0

        lax.fori_loop(0, BAND, turn, 0)
        top = None
        for first in parts:
            top = score(band, wide_q[rows_of(0), :], first, 0, top)
        tops[0][...] = top

        def go(i, _, band=band, between=between):
            for slot in range(2):
                attend(band, 2 * i + slot, slot, True)
                for n in range(slot, STEPS - 2, 2):
                    if between is not None:

                        @pl.when(i == n // 2)
                        def _(n=n):
                            between(n)

            return 0

        lax.fori_loop(0, STEPS // 2 - 1, go, 0)
        attend(band, STEPS - 2, 0, True)
        if between is not None:
            between(STEPS - 2)
        attend(band, STEPS - 1, 1, False)

    out[:, pl.ds(pl.multiple_of(head * (HEADS * VHEAD), 128), HEADS * VHEAD)] = attended[
        pl.ds(pl.multiple_of(head * 16, 16), 16), :
    ]
    for number in range(len(sent)):
        transfer(0, 0, 0, 0, twin, number, core).wait_send()

    def finish(step, _):
        for i in range(7):
            deliver(step, i).wait_send()
            sender = (head + 7 - i) % 8
            pltpu.make_async_remote_copy(
                src_ref=attended.at[pl.ds(0, 16), columns_of(0, step)],
                dst_ref=out.at[:, columns_of(sender, step)],
                send_sem=out_send.at[step, i], recv_sem=out_recv.at[step, i],
                device_id=mates[i], device_id_type=MESH,
            ).wait_recv()
        return 0

    lax.fori_loop(0, STEPS, finish, 0)


def shards(queries, latent_keys, w_key_up, w_value_up, slab_order, segment_ids):
    rows = HEADS * ROWS
    return pl.pallas_call(
        kernel,
        out_shape=jax.ShapeDtypeStruct((16, 8 * HEADS * VHEAD), BF16),
        in_specs=[
            pl.BlockSpec(memory_space=pltpu.SMEM),
            pl.BlockSpec(memory_space=pltpu.SMEM),
            pl.BlockSpec(memory_space=pltpu.VMEM),
            pl.BlockSpec(memory_space=pl.ANY),
            pl.BlockSpec(memory_space=pl.ANY),
            pl.BlockSpec(memory_space=pl.ANY),
        ],
        out_specs=pl.BlockSpec(memory_space=pltpu.VMEM),
        scratch_shapes=[
            pltpu.VMEM((BAND, WIDE, ROWS), BF16),
            pltpu.VMEM((BAND, WIDE, ROWS), BF16),
            pltpu.VMEM((BAND, WIDE, ROWS), BF16),
            pltpu.VMEM((BAND, WIDE, ROWS), BF16),
            pltpu.VMEM((rows, WIDE), BF16),
            pltpu.VMEM((BAND * ROWS, LATENT), BF16),
            pltpu.VMEM((PAIR, BAND * ROWS), F32),
            pltpu.VMEM((PAIR, BAND * ROWS), F32),
            pltpu.VMEM((PAIR, 128), F32),
            pltpu.VMEM((PAIR, 128), F32),
            pltpu.VMEM((rows, 128), F32),
            pltpu.VMEM((rows, 128), F32),
            pltpu.VMEM((rows, LATENT), F32),
            pltpu.VMEM((ROWS, HEADS * VHEAD), BF16),
            pltpu.VMEM((ROWS, HEADS * (NOPE + ROPE)), BF16),
            pltpu.VMEM((HEADS, NOPE, LATENT), BF16),
            pltpu.VMEM((HEADS, LATENT, VHEAD), BF16),
            pltpu.SemaphoreType.DMA((3,)),
            pltpu.SemaphoreType.DMA((64,)),
            pltpu.SemaphoreType.DMA((4, BAND, 2)),
            pltpu.SemaphoreType.DMA((STEPS, 7)),
            pltpu.SemaphoreType.DMA((STEPS, 7)),
        ],
        compiler_params=pltpu.CompilerParams(
            collective_id=0, has_side_effects=True, vmem_limit_bytes=56 * 2**20
        ),
        cost_estimate=pl.CostEstimate(
            flops=20 * 10**9, bytes_accessed=6 * 2**20, transcendentals=8 * 10**6
        ),
    )(slab_order, segment_ids, latent_keys.T, queries, w_key_up, w_value_up)


def solution(mesh):
    in_specs = (
        P("seq", "head"),
        P("seq", None),
        P("head", None, None),
        P("head", None, None),
        P(),
        P(),
    )
    out_specs = P(("seq", "head"), None)
    return jax.shard_map(shards, mesh=mesh, in_specs=in_specs, out_specs=out_specs, check_vma=False)
```

```python
import functools

import jax
import jax.numpy as jnp
from jax import lax
from jax.experimental import pallas as pl
from jax.experimental.pallas import tpu as pltpu
from jax.sharding import PartitionSpec as P

MESH = pl.DeviceIdType.MESH
BF16 = jnp.bfloat16
F32 = jnp.float32

HEADS = 16
ROWS = 128
NOPE, ROPE, LATENT, VHEAD = 128, 64, 512, 128
KEY = LATENT + ROPE
QUARTER = KEY // 4
WIDE = KEY + ROWS
SLABS = 32
BAND = 8
PAIR = 2 * ROWS
STEPS = HEADS // 2
CHUNK = 256
NEGATIVE = -1.0e30
LOG2E = 1.4426950408889634


def dot(a, b):
    return jnp.dot(a, b, preferred_element_type=F32)


def kernel(
    order, segment, latent, queries_hbm, w_key_hbm, w_value_hbm, out,
    own_band, outer_band, inner_band, far_band, wide_q, value, scores_0, scores_1, tops_0, tops_1, best, total, context,
    attended, queries, w_key, w_value, load_sem, send_sem, recv_sem, out_send, out_recv,
):
    seq, head = lax.axis_index("seq"), lax.axis_index("head")
    core, zh, x = seq % 2, (seq // 2) % 4, seq // 8
    y, zl = head % 4, head // 4

    def slab(x_of, zh_of, core_of):
        return (x_of * 4 + zh_of) * 2 + core_of

    x_up, x_down, x_far = (x + 1) % 4, (x + 3) % 4, (x + 2) % 4
    zh_outer = (zh + 3 + 2 * zl) % 4
    zh_inner = (zh + 5 - 2 * zl) % 4
    zh_far = (zh + 2) % 4
    up = (slab(x_up, zh, core), head)
    down = (slab(x_down, zh, core), head)
    outer = (slab(x, zh_outer, core), (1 - zl) * 4 + y)
    inner = (seq, (1 - zl) * 4 + y)
    beyond = (slab(x, zh_far, core), (1 - zl) * 4 + y)
    twin = (slab(x, zh, 1 - core), head)
    y_up = (seq, zl * 4 + (y + 1) % 4)
    y_down = (seq, zl * 4 + (y + 3) % 4)
    mates = [(seq, (head + 1 + i) % 8) for i in range(7)]

    loads = [
        pltpu.make_async_copy(queries_hbm, queries, load_sem.at[0]),
        pltpu.make_async_copy(w_key_hbm, w_key, load_sem.at[1]),
        pltpu.make_async_copy(w_value_hbm, w_value, load_sem.at[2]),
    ]
    for load in loads:
        load.start()
    bands = (own_band, outer_band, inner_band, far_band)
    own_band[core, :KEY] = latent[...]

    barrier = pltpu.get_barrier_semaphore()
    greeted = [up, down, outer, beyond, twin] + mates
    for device in greeted:
        pl.semaphore_signal(barrier, inc=1, device_id=device, device_id_type=MESH)
    pl.semaphore_wait(barrier, len(greeted))

    def transfer(band, landing, k, first, length, device, sent, core_of):
        there = (k + (3 if device is up else 1 if device is down else 0)) % 4
        span = pl.ds(pl.multiple_of(first * QUARTER, 16), length * QUARTER)
        return pltpu.make_async_remote_copy(
            src_ref=bands[band].at[2 * k + core_of, span],
            dst_ref=bands[landing].at[2 * there + core_of, span],
            send_sem=send_sem.at[sent], recv_sem=recv_sem.at[landing, 2 * there + core_of, first],
            device_id=device, device_id_type=MESH,
        )

    sent = []

    def send(band, landing, k, first, length, *devices):
        for device in devices:
            transfer(band, landing, k, first, length, device, len(sent), core).start()
            sent.append(length)

    def arrive(band, k, first, length, core_of=core):
        transfer(band, band, k, first, length, twin, 0, core_of).wait_recv()

    kept, other = 2 * (y % 2), 2 - 2 * (y % 2)
    for half in (0, 2):
        send(0, 0, 0, half, 2, up, down)
        send(0, 1, 0, half, 2, outer)
    send(0, 3, 0, 2 * zl, 2, beyond)
    send(0, 0, 0, 0, 4, twin)

    def search(_, span):
        low, high = span
        middle = (low + high) // 2
        first = segment[middle] == 0
        return jnp.where(first, middle + 1, low), jnp.where(first, high, middle)

    boundary, _ = lax.fori_loop(0, 12, search, (0, SLABS * ROWS - 1))
    my_slab = order[seq]

    loads[0].wait()
    loads[1].wait()
    row = lax.broadcasted_iota(jnp.int32, (ROWS, ROWS), 0)
    column = lax.broadcasted_iota(jnp.int32, (ROWS, ROWS), 1)
    one_hot = (row == column).astype(BF16)

    def absorb(j, _):
        two = queries[:, pl.ds(pl.multiple_of(j * 384, 384), 384)]
        for i in range(2):
            mine = two[:, i * 192 : i * 192 + 192]
            rows = pl.ds(pl.multiple_of((2 * j + i) * ROWS, ROWS), ROWS)
            wide_q[rows, :LATENT] = dot(mine[:, :NOPE], w_key[2 * j + i]).astype(BF16)
            wide_q[rows, LATENT:] = jnp.concatenate([mine[:, NOPE:], one_hot], axis=1)
        return 0

    lax.fori_loop(0, HEADS // 2, absorb, 0)

    query_pos = my_slab * ROWS + row
    first_live = jnp.where(query_pos >= boundary, boundary, 0)

    def cover(place, _):
        for band, zh_of in enumerate((zh, zh_outer, zh_inner, zh_far)):
            key_pos = order[slab((x + place // 2) % 4, zh_of, place % 2)] * ROWS + column
            live = (key_pos >= first_live) & (key_pos <= query_pos)
            bands[band][place, KEY:] = jnp.where(live, 0.0, NEGATIVE).astype(BF16)
        return 0

    lax.fori_loop(0, BAND, cover, 0)

    def own_near(k, onward, passed):
        arrive(0, k, 0, 2)
        arrive(0, k, 2, 2)
        send(0, 0, k, passed, 2, onward)
        send(0, 0, k, 0, 4, twin)

    def own_far():
        for half in (0, 2):
            arrive(0, 2, half, 2)
        send(0, 0, 2, 0, 4, twin)

    def next_door():
        for half in (0, 2):
            arrive(1, 0, half, 2)
            send(1, 2, 0, half, 2, inner)
        send(1, 1, 0, kept, 2, up, down)
        send(1, 1, 0, 0, 4, twin)

    def one_further():
        for half in (0, 2):
            arrive(2, 0, half, 2)
        send(2, 2, 0, kept, 2, up, down)
        send(2, 2, 0, 0, 4, twin)

    def from_beyond():
        arrive(3, 0, 2 - 2 * zl, 2)
        send(3, 3, 0, 2 - 2 * zl, 2, inner)

    def far_whole():
        arrive(3, 0, 2 * zl, 2)
        send(3, 3, 0, kept, 2, up, down)
        send(3, 3, 0, 0, 4, twin)

    def near(band):
        for k, onward, part, side in ((3, up, 0, y_up), (1, down, 1, y_down)):
            arrive(band, k, kept, 2)
            send(band, band, k, kept + part, 1, onward)
            send(band, band, k, kept, 2, side, twin)

    def far(band):
        for part, side in ((0, y_up), (1, y_down)):
            arrive(band, 2, kept + part, 1)
            send(band, band, 2, kept + part, 1, side)
        send(band, band, 2, kept, 2, twin)

    def side_near(band):
        for k in (3, 1):
            arrive(band, k, other, 2)
            send(band, band, k, other, 2, twin)

    def side_far(band):
        for part in range(2):
            arrive(band, 2, other + part, 1)
        send(band, band, 2, other, 2, twin)

    def complete(group):
        for band, k in group:
            if band == 0 or k == 0:
                arrive(band, k, 0, 4, 1 - core)
            else:
                for half in (0, 2):
                    arrive(band, k, half, 2, 1 - core)

    groups = (
        ((0, 0), (0, 3), (0, 1), (1, 0)),
        ((0, 2), (2, 0), (1, 3), (1, 1)),
        ((3, 0), (1, 2), (2, 3), (2, 1)),
        ((3, 3), (3, 1), (2, 2), (3, 2)),
    )
    polls = (
        {1: [from_beyond], 3: [own_far], 4: [one_further, lambda: near(1)], 6: [far_whole]},
        {
            0: [lambda: far(1)], 1: [lambda: near(2)], 3: [lambda: side_far(1), lambda: near(3)],
            5: [lambda: side_near(2)], 6: [lambda: far(2)],
        },
        {
            0: [lambda: far(3)], 1: [lambda: side_near(3)], 3: [lambda: side_far(2)],
            5: [lambda: side_far(3)],
        },
        {},
    )
    before_group = ([], [lambda: side_near(1)], [], [])

    next_door()
    own_near(3, up, 0)
    own_near(1, down, 2)

    scale = (NOPE + ROPE) ** -0.5 * LOG2E
    scores, tops = (scores_0, scores_1), (tops_0, tops_1)
    parts = range(0, BAND * ROWS, CHUNK)

    def rows_of(step):
        return pl.ds(pl.multiple_of(step * PAIR, PAIR), PAIR)

    def score(group, q, first, slot, top):
        band, k = groups[group][first // CHUNK]
        keys = jnp.concatenate([bands[band][2 * k], bands[band][2 * k + 1]], axis=1)
        s = dot(q, keys)
        scores[slot][:, pl.ds(first, CHUNK)] = s
        for i in range(0, CHUNK, 128):
            part = s[:, i : i + 128]
            top = part if top is None else jnp.maximum(top, part)
        return top

    def attend(group, step, slot, ahead):
        here = rows_of(step)
        top = jnp.broadcast_to(jnp.max(tops[slot][...], axis=1, keepdims=True), (PAIR, 128)) * scale
        if group == 0:
            sums = jnp.zeros((PAIR, 128), F32)
        else:
            before = best[here, :]
            top = jnp.maximum(top, before)
            fade = jnp.exp2(before - top)
            sums = total[here, :] * fade
        gained, next_top = None, None
        for first in parts:
            if ahead:
                next_top = score(group, wide_q[rows_of(step + 1), :], first, 1 - slot, next_top)
            weights = []
            for i in range(0, CHUNK, 128):
                w = jnp.exp2(scores[slot][:, pl.ds(first + i, 128)] * scale - top)
                sums = sums + w
                weights.append(w.astype(BF16))
            more = dot(jnp.concatenate(weights, axis=1), value[pl.ds(first, CHUNK), :])
            gained = more if gained is None else gained + more
        if ahead:
            tops[1 - slot][...] = next_top
        if group > 0:
            gained = gained + context[here, :] * jnp.concatenate([fade] * 4, axis=1)
        if group < 3:
            best[here, :] = top
            total[here, :] = sums
            context[here, :] = gained
            return
        finished = (gained / jnp.sum(sums, axis=1, keepdims=True)).astype(BF16)
        for i in range(2):
            h = 2 * step + i
            attended[:, pl.ds(pl.multiple_of(h * VHEAD, VHEAD), VHEAD)] = dot(
                finished[i * ROWS : (i + 1) * ROWS], w_value[h]
            ).astype(BF16)
        for i in range(7):
            deliver(step, i).start()

    def columns_of(who, step):
        return pl.ds(pl.multiple_of(who * (HEADS * VHEAD) + step * PAIR, PAIR), PAIR)

    def deliver(step, i):
        mate = mates[i][1]
        return pltpu.make_async_remote_copy(
            src_ref=attended.at[pl.ds(pl.multiple_of(mate * 16, 16), 16), columns_of(0, step)],
            dst_ref=out.at[:, columns_of(head, step)],
            send_sem=out_send.at[step, i], recv_sem=out_recv.at[step, i],
            device_id=mates[i], device_id_type=MESH,
        )

    for group in range(4):
        for wait in before_group[group]:
            wait()
        complete(groups[group])
        if group == 3:
            loads[2].wait()

        for i, (band, k) in enumerate(groups[group]):
            for c in range(2):
                taken = bands[band][2 * k + c, :LATENT]
                value[pl.ds((2 * i + c) * ROWS, ROWS), :] = taken.T
        top = None
        for first in parts:
            top = score(group, wide_q[rows_of(0), :], first, 0, top)
        tops[0][...] = top

        def go(i, _, group=group):
            for slot in range(2):
                attend(group, 2 * i + slot, slot, True)
                for n in range(slot, STEPS - 2, 2):
                    if n in polls[group]:

                        @pl.when(i == n // 2)
                        def _(n=n):
                            for wait in polls[group][n]:
                                wait()

            return 0

        lax.fori_loop(0, STEPS // 2 - 1, go, 0)
        attend(group, STEPS - 2, 0, True)
        for wait in polls[group].get(STEPS - 2, []):
            wait()
        attend(group, STEPS - 1, 1, False)

    out[:, pl.ds(pl.multiple_of(head * (HEADS * VHEAD), 128), HEADS * VHEAD)] = attended[
        pl.ds(pl.multiple_of(head * 16, 16), 16), :
    ]
    for number, length in enumerate(sent):
        transfer(0, 0, 0, 0, length, twin, number, core).wait_send()

    def finish(step, _):
        for i in range(7):
            deliver(step, i).wait_send()
            sender = (head + 7 - i) % 8
            pltpu.make_async_remote_copy(
                src_ref=attended.at[pl.ds(0, 16), columns_of(0, step)],
                dst_ref=out.at[:, columns_of(sender, step)],
                send_sem=out_send.at[step, i], recv_sem=out_recv.at[step, i],
                device_id=mates[i], device_id_type=MESH,
            ).wait_recv()
        return 0

    lax.fori_loop(0, STEPS, finish, 0)


def shards(queries, latent_keys, w_key_up, w_value_up, slab_order, segment_ids):
    rows = HEADS * ROWS
    return pl.pallas_call(
        kernel,
        out_shape=jax.ShapeDtypeStruct((16, 8 * HEADS * VHEAD), BF16),
        in_specs=[
            pl.BlockSpec(memory_space=pltpu.SMEM),
            pl.BlockSpec(memory_space=pltpu.SMEM),
            pl.BlockSpec(memory_space=pltpu.VMEM),
            pl.BlockSpec(memory_space=pl.ANY),
            pl.BlockSpec(memory_space=pl.ANY),
            pl.BlockSpec(memory_space=pl.ANY),
        ],
        out_specs=pl.BlockSpec(memory_space=pltpu.VMEM),
        scratch_shapes=[
            pltpu.VMEM((BAND, WIDE, ROWS), BF16),
            pltpu.VMEM((BAND, WIDE, ROWS), BF16),
            pltpu.VMEM((BAND, WIDE, ROWS), BF16),
            pltpu.VMEM((BAND, WIDE, ROWS), BF16),
            pltpu.VMEM((rows, WIDE), BF16),
            pltpu.VMEM((BAND * ROWS, LATENT), BF16),
            pltpu.VMEM((PAIR, BAND * ROWS), F32),
            pltpu.VMEM((PAIR, BAND * ROWS), F32),
            pltpu.VMEM((PAIR, 128), F32),
            pltpu.VMEM((PAIR, 128), F32),
            pltpu.VMEM((rows, 128), F32),
            pltpu.VMEM((rows, 128), F32),
            pltpu.VMEM((rows, LATENT), F32),
            pltpu.VMEM((ROWS, HEADS * VHEAD), BF16),
            pltpu.VMEM((ROWS, HEADS * (NOPE + ROPE)), BF16),
            pltpu.VMEM((HEADS, NOPE, LATENT), BF16),
            pltpu.VMEM((HEADS, LATENT, VHEAD), BF16),
            pltpu.SemaphoreType.DMA((3,)),
            pltpu.SemaphoreType.DMA((72,)),
            pltpu.SemaphoreType.DMA((4, BAND, 4)),
            pltpu.SemaphoreType.DMA((STEPS, 7)),
            pltpu.SemaphoreType.DMA((STEPS, 7)),
        ],
        compiler_params=pltpu.CompilerParams(
            collective_id=0, has_side_effects=True, vmem_limit_bytes=56 * 2**20
        ),
        cost_estimate=pl.CostEstimate(
            flops=20 * 10**9, bytes_accessed=6 * 2**20, transcendentals=8 * 10**6
        ),
    )(slab_order, segment_ids, latent_keys.T, queries, w_key_up, w_value_up)


def solution(mesh):
    in_specs = (
        P("seq", "head"),
        P("seq", None),
        P("head", None, None),
        P("head", None, None),
        P(),
        P(),
    )
    out_specs = P(("seq", "head"), None)
    return jax.shard_map(shards, mesh=mesh, in_specs=in_specs, out_specs=out_specs, check_vma=False)
```

```python
import functools

import jax
import jax.numpy as jnp
from jax import lax
from jax.experimental import pallas as pl
from jax.experimental.pallas import tpu as pltpu
from jax.sharding import PartitionSpec as P

MESH = pl.DeviceIdType.MESH
BF16 = jnp.bfloat16
F32 = jnp.float32

HEADS = 16
ROWS = 128
NOPE, ROPE, LATENT, VHEAD = 128, 64, 512, 128
KEY = LATENT + ROPE
QUARTER = KEY // 4
WIDE = KEY + ROWS
SLABS = 32
BAND = 8
PAIR = 2 * ROWS
STEPS = HEADS // 2
CHUNK = 256
NEGATIVE = -1.0e30
LOG2E = 1.4426950408889634


def dot(a, b):
    return jnp.dot(a, b, preferred_element_type=F32)


def kernel(
    order, segment, latent, queries_hbm, w_key_hbm, w_value_hbm, out,
    own_band, outer_band, inner_band, far_band, wide_q, value, scores_0, scores_1, tops_0, tops_1, best, total, context,
    attended, queries, w_key, w_value, load_sem, send_sem, recv_sem, out_send, out_recv,
):
    seq, head = lax.axis_index("seq"), lax.axis_index("head")
    core, zh, x = seq % 2, (seq // 2) % 4, seq // 8
    y, zl = head % 4, head // 4

    def slab(x_of, zh_of, core_of):
        return (x_of * 4 + zh_of) * 2 + core_of

    x_up, x_down, x_far = (x + 1) % 4, (x + 3) % 4, (x + 2) % 4
    zh_outer = (zh + 3 + 2 * zl) % 4
    zh_inner = (zh + 5 - 2 * zl) % 4
    zh_far = (zh + 2) % 4
    up = (slab(x_up, zh, core), head)
    down = (slab(x_down, zh, core), head)
    outer = (slab(x, zh_outer, core), (1 - zl) * 4 + y)
    inner = (seq, (1 - zl) * 4 + y)
    beyond = (slab(x, zh_far, core), (1 - zl) * 4 + y)
    twin = (slab(x, zh, 1 - core), head)
    y_up = (seq, zl * 4 + (y + 1) % 4)
    y_down = (seq, zl * 4 + (y + 3) % 4)
    mates = [(seq, (head + 1 + i) % 8) for i in range(7)]

    loads = [
        pltpu.make_async_copy(queries_hbm, queries, load_sem.at[0]),
        pltpu.make_async_copy(w_key_hbm, w_key, load_sem.at[1]),
        pltpu.make_async_copy(w_value_hbm, w_value, load_sem.at[2]),
    ]
    for load in loads:
        load.start()
    bands = (own_band, outer_band, inner_band, far_band)
    own_band[core, :KEY] = latent[...]

    barrier = pltpu.get_barrier_semaphore()
    greeted = [up, down, outer, beyond, twin] + mates
    for device in greeted:
        pl.semaphore_signal(barrier, inc=1, device_id=device, device_id_type=MESH)
    pl.semaphore_wait(barrier, len(greeted))

    def transfer(band, landing, k, first, length, device, sent, core_of):
        there = (k + (3 if device is up else 1 if device is down else 0)) % 4
        span = pl.ds(pl.multiple_of(first * QUARTER, 16), length * QUARTER)
        return pltpu.make_async_remote_copy(
            src_ref=bands[band].at[2 * k + core_of, span],
            dst_ref=bands[landing].at[2 * there + core_of, span],
            send_sem=send_sem.at[sent], recv_sem=recv_sem.at[landing, 2 * there + core_of, first],
            device_id=device, device_id_type=MESH,
        )

    sent = []

    def send(band, landing, k, first, length, *devices):
        for device in devices:
            transfer(band, landing, k, first, length, device, len(sent), core).start()
            sent.append(length)

    drained = []

    def drain(until):
        for number in range(len(drained), until):
            transfer(0, 0, 0, 0, sent[number], twin, number, core).wait_send()
            drained.append(number)

    def arrive(band, k, first, length, core_of=core):
        transfer(band, band, k, first, length, twin, 0, core_of).wait_recv()

    kept, other = 2 * (y % 2), 2 - 2 * (y % 2)
    for half in (0, 2):
        send(0, 0, 0, half, 2, up, down)
        send(0, 1, 0, half, 2, outer)
    send(0, 3, 0, 2 * zl, 2, beyond)
    send(0, 0, 0, 0, 4, twin)

    def search(_, span):
        low, high = span
        middle = (low + high) // 2
        first = segment[middle] == 0
        return jnp.where(first, middle + 1, low), jnp.where(first, high, middle)

    boundary, _ = lax.fori_loop(0, 12, search, (0, SLABS * ROWS - 1))
    my_slab = order[seq]

    loads[0].wait()
    loads[1].wait()
    row = lax.broadcasted_iota(jnp.int32, (ROWS, ROWS), 0)
    column = lax.broadcasted_iota(jnp.int32, (ROWS, ROWS), 1)
    one_hot = (row == column).astype(BF16)

    def absorb(j, _):
        two = queries[:, pl.ds(pl.multiple_of(j * 384, 384), 384)]
        for i in range(2):
            mine = two[:, i * 192 : i * 192 + 192]
            rows = pl.ds(pl.multiple_of((2 * j + i) * ROWS, ROWS), ROWS)
            wide_q[rows, :LATENT] = dot(mine[:, :NOPE], w_key[2 * j + i]).astype(BF16)
            wide_q[rows, LATENT:] = jnp.concatenate([mine[:, NOPE:], one_hot], axis=1)
        return 0

    lax.fori_loop(0, HEADS // 2, absorb, 0)

    query_pos = my_slab * ROWS + row
    first_live = jnp.where(query_pos >= boundary, boundary, 0)

    def cover(place, _):
        for band, zh_of in enumerate((zh, zh_outer, zh_inner, zh_far)):
            key_pos = order[slab((x + place // 2) % 4, zh_of, place % 2)] * ROWS + column
            live = (key_pos >= first_live) & (key_pos <= query_pos)
            bands[band][place, KEY:] = jnp.where(live, 0.0, NEGATIVE).astype(BF16)
        return 0

    lax.fori_loop(0, BAND, cover, 0)

    def own_near(k, onward, passed):
        arrive(0, k, 0, 2)
        arrive(0, k, 2, 2)
        send(0, 0, k, passed, 2, onward)
        send(0, 0, k, 0, 4, twin)

    def own_far():
        for half in (0, 2):
            arrive(0, 2, half, 2)
        send(0, 0, 2, 0, 4, twin)

    def next_door():
        for half in (0, 2):
            arrive(1, 0, half, 2)
            send(1, 2, 0, half, 2, inner)
        send(1, 1, 0, kept, 2, up, down)
        send(1, 1, 0, 0, 4, twin)

    def one_further():
        for half in (0, 2):
            arrive(2, 0, half, 2)
        send(2, 2, 0, kept, 2, up, down)
        send(2, 2, 0, 0, 4, twin)

    def from_beyond():
        arrive(3, 0, 2 - 2 * zl, 2)
        send(3, 3, 0, 2 - 2 * zl, 2, inner)

    def far_whole():
        arrive(3, 0, 2 * zl, 2)
        send(3, 3, 0, kept, 2, up, down)
        send(3, 3, 0, 0, 4, twin)

    def near(band):
        for k, onward, part, side in ((3, up, 0, y_up), (1, down, 1, y_down)):
            arrive(band, k, kept, 2)
            send(band, band, k, kept + part, 1, onward)
            send(band, band, k, kept, 2, side, twin)

    def far(band):
        for part, side in ((0, y_up), (1, y_down)):
            arrive(band, 2, kept + part, 1)
            send(band, band, 2, kept + part, 1, side)
        send(band, band, 2, kept, 2, twin)

    def side_near(band):
        for k in (3, 1):
            arrive(band, k, other, 2)
            send(band, band, k, other, 2, twin)

    def side_far(band):
        for part in range(2):
            arrive(band, 2, other + part, 1)
        send(band, band, 2, other, 2, twin)

    def complete(group):
        for band, k in group:
            if band == 0 or k == 0:
                arrive(band, k, 0, 4, 1 - core)
            else:
                for half in (0, 2):
                    arrive(band, k, half, 2, 1 - core)

    groups = (
        ((0, 0), (0, 3), (0, 1), (1, 0)),
        ((0, 2), (2, 0), (1, 3), (1, 1)),
        ((3, 0), (1, 2), (2, 3), (2, 1)),
        ((3, 3), (3, 1), (2, 2), (3, 2)),
    )
    polls = (
        {0: [from_beyond], 2: [lambda: near(1)], 3: [own_far], 4: [one_further], 5: [far_whole], 6: [lambda: far(1)]},
        {
            0: [lambda: near(2)], 1: [lambda: side_far(1), lambda: near(3)],
            3: [lambda: far(2)], 4: [lambda: side_near(2), lambda: far(3)],
            5: [lambda: side_near(3)], 6: [lambda: side_far(2)],
        },
        {1: [lambda: side_far(3)]},
        {},
    )
    before_group = ([], [lambda: side_near(1)], [], [])

    next_door()
    own_near(3, up, 0)
    own_near(1, down, 2)

    scale = (NOPE + ROPE) ** -0.5 * LOG2E
    scores, tops = (scores_0, scores_1), (tops_0, tops_1)
    parts = range(0, BAND * ROWS, CHUNK)

    def rows_of(step):
        return pl.ds(pl.multiple_of(step * PAIR, PAIR), PAIR)

    def score(group, q, first, slot, top):
        band, k = groups[group][first // CHUNK]
        keys = jnp.concatenate([bands[band][2 * k], bands[band][2 * k + 1]], axis=1)
        s = dot(q, keys)
        scores[slot][:, pl.ds(first, CHUNK)] = s
        for i in range(0, CHUNK, 128):
            part = s[:, i : i + 128]
            top = part if top is None else jnp.maximum(top, part)
        return top

    def attend(group, step, slot, ahead):
        here = rows_of(step)
        top = jnp.broadcast_to(jnp.max(tops[slot][...], axis=1, keepdims=True), (PAIR, 128)) * scale
        if group == 0:
            sums = jnp.zeros((PAIR, 128), F32)
        else:
            before = best[here, :]
            top = jnp.maximum(top, before)
            fade = jnp.exp2(before - top)
            sums = total[here, :] * fade
        gained, next_top = None, None
        for first in parts:
            if ahead:
                next_top = score(group, wide_q[rows_of(step + 1), :], first, 1 - slot, next_top)
            weights = []
            for i in range(0, CHUNK, 128):
                w = jnp.exp2(scores[slot][:, pl.ds(first + i, 128)] * scale - top)
                sums = sums + w
                weights.append(w.astype(BF16))
            more = dot(jnp.concatenate(weights, axis=1), value[pl.ds(first, CHUNK), :])
            gained = more if gained is None else gained + more
        if ahead:
            tops[1 - slot][...] = next_top
        if group > 0:
            gained = gained + context[here, :] * jnp.concatenate([fade] * 4, axis=1)
        if group < 3:
            best[here, :] = top
            total[here, :] = sums
            context[here, :] = gained
            return
        finished = (gained / jnp.sum(sums, axis=1, keepdims=True)).astype(BF16)
        for i in range(2):
            h = 2 * step + i
            attended[:, pl.ds(pl.multiple_of(h * VHEAD, VHEAD), VHEAD)] = dot(
                finished[i * ROWS : (i + 1) * ROWS], w_value[h]
            ).astype(BF16)
        for i in range(7):
            deliver(step, i).start()

    def columns_of(who, step):
        return pl.ds(pl.multiple_of(who * (HEADS * VHEAD) + step * PAIR, PAIR), PAIR)

    def deliver(step, i):
        mate = mates[i][1]
        return pltpu.make_async_remote_copy(
            src_ref=attended.at[pl.ds(pl.multiple_of(mate * 16, 16), 16), columns_of(0, step)],
            dst_ref=out.at[:, columns_of(head, step)],
            send_sem=out_send.at[i], recv_sem=out_recv.at[i],
            device_id=mates[i], device_id_type=MESH,
        )

    for group in range(4):
        for wait in before_group[group]:
            wait()
        complete(groups[group])
        if group == 3:
            loads[2].wait()

        for i, (band, k) in enumerate(groups[group]):
            for c in range(2):
                taken = bands[band][2 * k + c, :LATENT]
                value[pl.ds((2 * i + c) * ROWS, ROWS), :] = taken.T
        top = None
        for first in parts:
            top = score(group, wide_q[rows_of(0), :], first, 0, top)
        tops[0][...] = top

        def go(i, _, group=group):
            for slot in range(2):
                attend(group, 2 * i + slot, slot, True)
                for n in range(slot, STEPS - 2, 2):
                    if n in polls[group]:

                        @pl.when(i == n // 2)
                        def _(n=n):
                            for wait in polls[group][n]:
                                wait()

            return 0

        lax.fori_loop(0, STEPS // 2 - 1, go, 0)
        attend(group, STEPS - 2, 0, True)
        for wait in polls[group].get(STEPS - 2, []):
            wait()
        attend(group, STEPS - 1, 1, False)

    out[:, pl.ds(pl.multiple_of(head * (HEADS * VHEAD), 128), HEADS * VHEAD)] = attended[
        pl.ds(pl.multiple_of(head * 16, 16), 16), :
    ]
    drain(len(sent))
    for i in range(7):
        mate, sender = mates[i][1], (head + 7 - i) % 8
        whole = pltpu.make_async_remote_copy(
            src_ref=attended.at[pl.ds(pl.multiple_of(mate * 16, 16), 16), :],
            dst_ref=out.at[:, pl.ds(pl.multiple_of(sender * (HEADS * VHEAD), 128), HEADS * VHEAD)],
            send_sem=out_send.at[i], recv_sem=out_recv.at[i],
            device_id=mates[i], device_id_type=MESH,
        )
        whole.wait_send()
        whole.wait_recv()


def shards(queries, latent_keys, w_key_up, w_value_up, slab_order, segment_ids):
    rows = HEADS * ROWS
    return pl.pallas_call(
        kernel,
        out_shape=jax.ShapeDtypeStruct((16, 8 * HEADS * VHEAD), BF16),
        in_specs=[
            pl.BlockSpec(memory_space=pltpu.SMEM),
            pl.BlockSpec(memory_space=pltpu.SMEM),
            pl.BlockSpec(memory_space=pltpu.VMEM),
            pl.BlockSpec(memory_space=pl.ANY),
            pl.BlockSpec(memory_space=pl.ANY),
            pl.BlockSpec(memory_space=pl.ANY),
        ],
        out_specs=pl.BlockSpec(memory_space=pltpu.VMEM),
        scratch_shapes=[
            pltpu.VMEM((BAND, WIDE, ROWS), BF16),
            pltpu.VMEM((BAND, WIDE, ROWS), BF16),
            pltpu.VMEM((BAND, WIDE, ROWS), BF16),
            pltpu.VMEM((BAND, WIDE, ROWS), BF16),
            pltpu.VMEM((rows, WIDE), BF16),
            pltpu.VMEM((BAND * ROWS, LATENT), BF16),
            pltpu.VMEM((PAIR, BAND * ROWS), F32),
            pltpu.VMEM((PAIR, BAND * ROWS), F32),
            pltpu.VMEM((PAIR, 128), F32),
            pltpu.VMEM((PAIR, 128), F32),
            pltpu.VMEM((rows, 128), F32),
            pltpu.VMEM((rows, 128), F32),
            pltpu.VMEM((rows, LATENT), F32),
            pltpu.VMEM((ROWS, HEADS * VHEAD), BF16),
            pltpu.VMEM((ROWS, HEADS * (NOPE + ROPE)), BF16),
            pltpu.VMEM((HEADS, NOPE, LATENT), BF16),
            pltpu.VMEM((HEADS, LATENT, VHEAD), BF16),
            pltpu.SemaphoreType.DMA((3,)),
            pltpu.SemaphoreType.DMA((72,)),
            pltpu.SemaphoreType.DMA((4, BAND, 4)),
            pltpu.SemaphoreType.DMA((7,)),
            pltpu.SemaphoreType.DMA((7,)),
        ],
        compiler_params=pltpu.CompilerParams(
            collective_id=0, has_side_effects=True, vmem_limit_bytes=56 * 2**20
        ),
        cost_estimate=pl.CostEstimate(
            flops=20 * 10**9, bytes_accessed=6 * 2**20, transcendentals=8 * 10**6
        ),
    )(slab_order, segment_ids, latent_keys.T, queries, w_key_up, w_value_up)


def solution(mesh):
    in_specs = (
        P("seq", "head"),
        P("seq", None),
        P("head", None, None),
        P("head", None, None),
        P(),
        P(),
    )
    out_specs = P(("seq", "head"), None)
    return jax.shard_map(shards, mesh=mesh, in_specs=in_specs, out_specs=out_specs, check_vma=False)
```

```python
import functools

import jax
import jax.numpy as jnp
from jax import lax
from jax.experimental import pallas as pl
from jax.experimental.pallas import tpu as pltpu
from jax.sharding import PartitionSpec as P

MESH = pl.DeviceIdType.MESH
BF16 = jnp.bfloat16
F32 = jnp.float32

HEADS = 16
ROWS = 128
NOPE, ROPE, LATENT, VHEAD = 128, 64, 512, 128
KEY = LATENT + ROPE
QUARTER = KEY // 4
WIDE = KEY + ROWS
SLABS = 32
BAND = 8
PAIR = 2 * ROWS
STEPS = HEADS // 2
CHUNK = 256
NEGATIVE = -1.0e30
LOG2E = 1.4426950408889634


def dot(a, b):
    return jnp.dot(a, b, preferred_element_type=F32)


def kernel(
    order, segment, latent, queries_hbm, w_key_hbm, w_value_hbm, out,
    own_band, outer_band, inner_band, far_band, wide_q, value, scores_0, scores_1, tops_0, tops_1, best, total, context,
    attended, queries, w_key, w_value, load_sem, send_sem, recv_sem, out_send, out_recv,
):
    seq, head = lax.axis_index("seq"), lax.axis_index("head")
    core, zh, x = seq % 2, (seq // 2) % 4, seq // 8
    y, zl = head % 4, head // 4

    def slab(x_of, zh_of, core_of):
        return (x_of * 4 + zh_of) * 2 + core_of

    x_up, x_down, x_far = (x + 1) % 4, (x + 3) % 4, (x + 2) % 4
    zh_outer = (zh + 3 + 2 * zl) % 4
    zh_inner = (zh + 5 - 2 * zl) % 4
    zh_far = (zh + 2) % 4
    up = (slab(x_up, zh, core), head)
    down = (slab(x_down, zh, core), head)
    outer = (slab(x, zh_outer, core), (1 - zl) * 4 + y)
    inner = (seq, (1 - zl) * 4 + y)
    beyond = (slab(x, zh_far, core), (1 - zl) * 4 + y)
    twin = (slab(x, zh, 1 - core), head)
    y_up = (seq, zl * 4 + (y + 1) % 4)
    y_down = (seq, zl * 4 + (y + 3) % 4)
    mates = [(seq, (head + 1 + i) % 8) for i in range(7)]

    loads = [
        pltpu.make_async_copy(queries_hbm, queries, load_sem.at[0]),
        pltpu.make_async_copy(w_key_hbm, w_key, load_sem.at[1]),
        pltpu.make_async_copy(w_value_hbm, w_value, load_sem.at[2]),
    ]
    for load in loads:
        load.start()
    bands = (own_band, outer_band, inner_band, far_band)
    own_band[core, :KEY] = latent[...]

    barrier = pltpu.get_barrier_semaphore()
    greeted = [up, down, outer, beyond, twin] + mates
    for device in greeted:
        pl.semaphore_signal(barrier, inc=1, device_id=device, device_id_type=MESH)
    pl.semaphore_wait(barrier, len(greeted))

    def transfer(band, landing, k, first, length, device, sent, core_of):
        there = (k + (3 if device is up else 1 if device is down else 0)) % 4
        span = pl.ds(pl.multiple_of(first * QUARTER, 16), length * QUARTER)
        return pltpu.make_async_remote_copy(
            src_ref=bands[band].at[2 * k + core_of, span],
            dst_ref=bands[landing].at[2 * there + core_of, span],
            send_sem=send_sem.at[sent], recv_sem=recv_sem.at[landing, 2 * there + core_of, first],
            device_id=device, device_id_type=MESH,
        )

    sent = []

    def send(band, landing, k, first, length, *devices):
        for device in devices:
            transfer(band, landing, k, first, length, device, len(sent), core).start()
            sent.append(length)

    drained = []

    def drain(until):
        for number in range(len(drained), until):
            transfer(0, 0, 0, 0, sent[number], twin, number, core).wait_send()
            drained.append(number)

    def arrive(band, k, first, length, core_of=core):
        transfer(band, band, k, first, length, twin, 0, core_of).wait_recv()

    kept, other = 2 * (y % 2), 2 - 2 * (y % 2)
    for half in (0, 2):
        send(0, 0, 0, half, 2, up, down)
    for half in (kept, other):
        send(0, 1, 0, half, 2, outer)
    send(0, 3, 0, 2 * zl, 2, beyond)
    send(0, 0, 0, 0, 4, twin)

    def search(_, span):
        low, high = span
        middle = (low + high) // 2
        first = segment[middle] == 0
        return jnp.where(first, middle + 1, low), jnp.where(first, high, middle)

    boundary, _ = lax.fori_loop(0, 12, search, (0, SLABS * ROWS - 1))
    my_slab = order[seq]

    loads[0].wait()
    loads[1].wait()
    row = lax.broadcasted_iota(jnp.int32, (ROWS, ROWS), 0)
    column = lax.broadcasted_iota(jnp.int32, (ROWS, ROWS), 1)
    one_hot = (row == column).astype(BF16)

    def absorb(j, _):
        two = queries[:, pl.ds(pl.multiple_of(j * 384, 384), 384)]
        for i in range(2):
            mine = two[:, i * 192 : i * 192 + 192]
            rows = pl.ds(pl.multiple_of((2 * j + i) * ROWS, ROWS), ROWS)
            wide_q[rows, :LATENT] = dot(mine[:, :NOPE], w_key[2 * j + i]).astype(BF16)
            wide_q[rows, LATENT:] = jnp.concatenate([mine[:, NOPE:], one_hot], axis=1)
        return 0

    lax.fori_loop(0, HEADS // 2, absorb, 0)

    query_pos = my_slab * ROWS + row
    first_live = jnp.where(query_pos >= boundary, boundary, 0)

    def cover(place, _):
        for band, zh_of in enumerate((zh, zh_outer, zh_inner, zh_far)):
            key_pos = order[slab((x + place // 2) % 4, zh_of, place % 2)] * ROWS + column
            live = (key_pos >= first_live) & (key_pos <= query_pos)
            bands[band][place, KEY:] = jnp.where(live, 0.0, NEGATIVE).astype(BF16)
        return 0

    lax.fori_loop(0, BAND, cover, 0)

    def own_near(k, onward, passed):
        arrive(0, k, 0, 2)
        arrive(0, k, 2, 2)
        send(0, 0, k, passed, 2, onward)
        send(0, 0, k, 0, 4, twin)

    def own_far():
        for half in (0, 2):
            arrive(0, 2, half, 2)
        send(0, 0, 2, 0, 4, twin)

    def next_door():
        arrive(1, 0, kept, 2)
        send(1, 1, 0, kept, 2, up, down)
        send(1, 2, 0, kept, 2, inner)
        arrive(1, 0, other, 2)
        send(1, 2, 0, other, 2, inner)
        send(1, 1, 0, 0, 4, twin)

    def one_further():
        arrive(2, 0, kept, 2)
        send(2, 2, 0, kept, 2, up, down)
        arrive(2, 0, other, 2)
        send(2, 2, 0, 0, 4, twin)

    def from_beyond():
        arrive(3, 0, 2 - 2 * zl, 2)
        send(3, 3, 0, 2 - 2 * zl, 2, inner)

    def far_whole():
        arrive(3, 0, 2 * zl, 2)
        send(3, 3, 0, kept, 2, up, down)
        send(3, 3, 0, 0, 4, twin)

    def near(band):
        for k, onward, part, side in ((3, up, 0, y_up), (1, down, 1, y_down)):
            arrive(band, k, kept, 2)
            send(band, band, k, kept + part, 1, onward)
            send(band, band, k, kept, 2, side, twin)

    def far(band):
        for part, side in ((0, y_up), (1, y_down)):
            arrive(band, 2, kept + part, 1)
            send(band, band, 2, kept + part, 1, side)
        send(band, band, 2, kept, 2, twin)

    def side_near(band):
        for k in (3, 1):
            arrive(band, k, other, 2)
            send(band, band, k, other, 2, twin)

    def side_far(band):
        for part in range(2):
            arrive(band, 2, other + part, 1)
        send(band, band, 2, other, 2, twin)

    def complete(group):
        for band, k in group:
            if band == 0 or k == 0:
                arrive(band, k, 0, 4, 1 - core)
            else:
                for half in (0, 2):
                    arrive(band, k, half, 2, 1 - core)

    groups = (
        ((0, 0), (0, 3), (0, 1), (1, 0)),
        ((0, 2), (2, 0), (1, 3), (1, 1)),
        ((3, 0), (1, 2), (2, 3), (2, 1)),
        ((3, 3), (3, 1), (2, 2), (3, 2)),
    )
    polls = (
        {0: [from_beyond], 2: [lambda: near(1)], 3: [own_far], 4: [one_further], 5: [far_whole], 6: [lambda: far(1)]},
        {
            0: [lambda: near(2)], 1: [lambda: side_far(1), lambda: near(3)],
            3: [lambda: far(2)], 4: [lambda: side_near(2), lambda: far(3)],
            5: [lambda: side_near(3)], 6: [lambda: side_far(2)],
        },
        {1: [lambda: side_far(3)]},
        {},
    )
    before_group = ([], [lambda: side_near(1)], [], [])

    next_door()
    own_near(3, up, 0)
    own_near(1, down, 2)

    scale = (NOPE + ROPE) ** -0.5 * LOG2E
    scores, tops = (scores_0, scores_1), (tops_0, tops_1)
    parts = range(0, BAND * ROWS, CHUNK)

    def rows_of(step):
        return pl.ds(pl.multiple_of(step * PAIR, PAIR), PAIR)

    def score(group, q, first, slot, top):
        band, k = groups[group][first // CHUNK]
        keys = jnp.concatenate([bands[band][2 * k], bands[band][2 * k + 1]], axis=1)
        s = dot(q, keys)
        scores[slot][:, pl.ds(first, CHUNK)] = s
        for i in range(0, CHUNK, 128):
            part = s[:, i : i + 128]
            top = part if top is None else jnp.maximum(top, part)
        return top

    def attend(group, step, slot, ahead):
        here = rows_of(step)
        top = jnp.broadcast_to(jnp.max(tops[slot][...], axis=1, keepdims=True), (PAIR, 128)) * scale
        if group == 0:
            sums = jnp.zeros((PAIR, 128), F32)
        else:
            before = best[here, :]
            top = jnp.maximum(top, before)
            fade = jnp.exp2(before - top)
            sums = total[here, :] * fade
        gained, next_top = None, None
        for first in parts:
            if ahead:
                next_top = score(group, wide_q[rows_of(step + 1), :], first, 1 - slot, next_top)
            weights = []
            for i in range(0, CHUNK, 128):
                w = jnp.exp2(scores[slot][:, pl.ds(first + i, 128)] * scale - top)
                sums = sums + w
                weights.append(w.astype(BF16))
            more = dot(jnp.concatenate(weights, axis=1), value[pl.ds(first, CHUNK), :])
            gained = more if gained is None else gained + more
        if ahead:
            tops[1 - slot][...] = next_top
        if group > 0:
            gained = gained + context[here, :] * jnp.concatenate([fade] * 4, axis=1)
        if group < 3:
            best[here, :] = top
            total[here, :] = sums
            context[here, :] = gained
            return
        finished = (gained / jnp.sum(sums, axis=1, keepdims=True)).astype(BF16)
        for i in range(2):
            h = 2 * step + i
            attended[:, pl.ds(pl.multiple_of(h * VHEAD, VHEAD), VHEAD)] = dot(
                finished[i * ROWS : (i + 1) * ROWS], w_value[h]
            ).astype(BF16)
        for i in range(7):
            deliver(step, i).start()

    def columns_of(who, step):
        return pl.ds(pl.multiple_of(who * (HEADS * VHEAD) + step * PAIR, PAIR), PAIR)

    def deliver(step, i):
        mate = mates[i][1]
        return pltpu.make_async_remote_copy(
            src_ref=attended.at[pl.ds(pl.multiple_of(mate * 16, 16), 16), columns_of(0, step)],
            dst_ref=out.at[:, columns_of(head, step)],
            send_sem=out_send.at[i], recv_sem=out_recv.at[i],
            device_id=mates[i], device_id_type=MESH,
        )

    for group in range(4):
        for wait in before_group[group]:
            wait()
        complete(groups[group])
        if group == 3:
            loads[2].wait()

        for i, (band, k) in enumerate(groups[group]):
            for c in range(2):
                taken = bands[band][2 * k + c, :LATENT]
                value[pl.ds((2 * i + c) * ROWS, ROWS), :] = taken.T
        top = None
        for first in parts:
            top = score(group, wide_q[rows_of(0), :], first, 0, top)
        tops[0][...] = top

        def go(i, _, group=group):
            for slot in range(2):
                attend(group, 2 * i + slot, slot, True)
                for n in range(slot, STEPS - 2, 2):
                    if n in polls[group]:

                        @pl.when(i == n // 2)
                        def _(n=n):
                            for wait in polls[group][n]:
                                wait()

            return 0

        lax.fori_loop(0, STEPS // 2 - 1, go, 0)
        attend(group, STEPS - 2, 0, True)
        for wait in polls[group].get(STEPS - 2, []):
            wait()
        attend(group, STEPS - 1, 1, False)

    out[:, pl.ds(pl.multiple_of(head * (HEADS * VHEAD), 128), HEADS * VHEAD)] = attended[
        pl.ds(pl.multiple_of(head * 16, 16), 16), :
    ]
    drain(len(sent))
    for i in range(7):
        mate, sender = mates[i][1], (head + 7 - i) % 8
        whole = pltpu.make_async_remote_copy(
            src_ref=attended.at[pl.ds(pl.multiple_of(mate * 16, 16), 16), :],
            dst_ref=out.at[:, pl.ds(pl.multiple_of(sender * (HEADS * VHEAD), 128), HEADS * VHEAD)],
            send_sem=out_send.at[i], recv_sem=out_recv.at[i],
            device_id=mates[i], device_id_type=MESH,
        )
        whole.wait_send()
        whole.wait_recv()


def shards(queries, latent_keys, w_key_up, w_value_up, slab_order, segment_ids):
    rows = HEADS * ROWS
    return pl.pallas_call(
        kernel,
        out_shape=jax.ShapeDtypeStruct((16, 8 * HEADS * VHEAD), BF16),
        in_specs=[
            pl.BlockSpec(memory_space=pltpu.SMEM),
            pl.BlockSpec(memory_space=pltpu.SMEM),
            pl.BlockSpec(memory_space=pltpu.VMEM),
            pl.BlockSpec(memory_space=pl.ANY),
            pl.BlockSpec(memory_space=pl.ANY),
            pl.BlockSpec(memory_space=pl.ANY),
        ],
        out_specs=pl.BlockSpec(memory_space=pltpu.VMEM),
        scratch_shapes=[
            pltpu.VMEM((BAND, WIDE, ROWS), BF16),
            pltpu.VMEM((BAND, WIDE, ROWS), BF16),
            pltpu.VMEM((BAND, WIDE, ROWS), BF16),
            pltpu.VMEM((BAND, WIDE, ROWS), BF16),
            pltpu.VMEM((rows, WIDE), BF16),
            pltpu.VMEM((BAND * ROWS, LATENT), BF16),
            pltpu.VMEM((PAIR, BAND * ROWS), F32),
            pltpu.VMEM((PAIR, BAND * ROWS), F32),
            pltpu.VMEM((PAIR, 128), F32),
            pltpu.VMEM((PAIR, 128), F32),
            pltpu.VMEM((rows, 128), F32),
            pltpu.VMEM((rows, 128), F32),
            pltpu.VMEM((rows, LATENT), F32),
            pltpu.VMEM((ROWS, HEADS * VHEAD), BF16),
            pltpu.VMEM((ROWS, HEADS * (NOPE + ROPE)), BF16),
            pltpu.VMEM((HEADS, NOPE, LATENT), BF16),
            pltpu.VMEM((HEADS, LATENT, VHEAD), BF16),
            pltpu.SemaphoreType.DMA((3,)),
            pltpu.SemaphoreType.DMA((72,)),
            pltpu.SemaphoreType.DMA((4, BAND, 4)),
            pltpu.SemaphoreType.DMA((7,)),
            pltpu.SemaphoreType.DMA((7,)),
        ],
        compiler_params=pltpu.CompilerParams(
            collective_id=0, has_side_effects=True, vmem_limit_bytes=56 * 2**20
        ),
        cost_estimate=pl.CostEstimate(
            flops=20 * 10**9, bytes_accessed=6 * 2**20, transcendentals=8 * 10**6
        ),
    )(slab_order, segment_ids, latent_keys.T, queries, w_key_up, w_value_up)


def solution(mesh):
    in_specs = (
        P("seq", "head"),
        P("seq", None),
        P("head", None, None),
        P("head", None, None),
        P(),
        P(),
    )
    out_specs = P(("seq", "head"), None)
    return jax.shard_map(shards, mesh=mesh, in_specs=in_specs, out_specs=out_specs, check_vma=False)
```

```python
import functools

import jax
import jax.numpy as jnp
from jax import lax
from jax.experimental import pallas as pl
from jax.experimental.pallas import tpu as pltpu
from jax.sharding import PartitionSpec as P

MESH = pl.DeviceIdType.MESH
BF16 = jnp.bfloat16
F32 = jnp.float32

HEADS = 16
ROWS = 128
NOPE, ROPE, LATENT, VHEAD = 128, 64, 512, 128
KEY = LATENT + ROPE
QUARTER = KEY // 4
WIDE = KEY + ROWS
SLABS = 32
BAND = 8
PAIR = 2 * ROWS
STEPS = HEADS // 2
CHUNK = 256
NEGATIVE = -1.0e30
LOG2E = 1.4426950408889634


def dot(a, b):
    return jnp.dot(a, b, preferred_element_type=F32)


def kernel(
    order, segment, latent, queries_hbm, w_key_hbm, w_value_hbm, out,
    own_band, outer_band, inner_band, far_band, wide_q, value, scores_0, scores_1, tops_0, tops_1, best, total, context,
    attended, queries, w_key, w_value, load_sem, send_sem, recv_sem, out_send, out_recv,
):
    seq, head = lax.axis_index("seq"), lax.axis_index("head")
    core, zh, x = seq % 2, (seq // 2) % 4, seq // 8
    y, zl = head % 4, head // 4

    def slab(x_of, zh_of, core_of):
        return (x_of * 4 + zh_of) * 2 + core_of

    x_up, x_down, x_far = (x + 1) % 4, (x + 3) % 4, (x + 2) % 4
    zh_outer = (zh + 3 + 2 * zl) % 4
    zh_inner = (zh + 5 - 2 * zl) % 4
    zh_far = (zh + 2) % 4
    up = (slab(x_up, zh, core), head)
    down = (slab(x_down, zh, core), head)
    outer = (slab(x, zh_outer, core), (1 - zl) * 4 + y)
    inner = (seq, (1 - zl) * 4 + y)
    beyond = (slab(x, zh_far, core), (1 - zl) * 4 + y)
    twin = (slab(x, zh, 1 - core), head)
    y_up = (seq, zl * 4 + (y + 1) % 4)
    y_down = (seq, zl * 4 + (y + 3) % 4)
    mates = [(seq, (head + 1 + i) % 8) for i in range(7)]

    loads = [
        pltpu.make_async_copy(queries_hbm, queries, load_sem.at[0]),
        pltpu.make_async_copy(w_key_hbm, w_key, load_sem.at[1]),
        pltpu.make_async_copy(w_value_hbm, w_value, load_sem.at[2]),
    ]
    for load in loads:
        load.start()
    bands = (own_band, outer_band, inner_band, far_band)
    own_band[core, :KEY] = latent[...]

    barrier = pltpu.get_barrier_semaphore()
    greeted = [up, down, outer, beyond, twin] + mates
    for device in greeted:
        pl.semaphore_signal(barrier, inc=1, device_id=device, device_id_type=MESH)
    pl.semaphore_wait(barrier, len(greeted))

    def transfer(band, landing, k, first, length, device, sent, core_of):
        there = (k + (3 if device is up else 1 if device is down else 0)) % 4
        span = pl.ds(pl.multiple_of(first * QUARTER, 16), length * QUARTER)
        return pltpu.make_async_remote_copy(
            src_ref=bands[band].at[2 * k + core_of, span],
            dst_ref=bands[landing].at[2 * there + core_of, span],
            send_sem=send_sem.at[sent], recv_sem=recv_sem.at[landing, 2 * there + core_of, first],
            device_id=device, device_id_type=MESH,
        )

    sent = []

    def send(band, landing, k, first, length, *devices):
        for device in devices:
            transfer(band, landing, k, first, length, device, len(sent), core).start()
            sent.append(length)

    drained = []

    def drain(until):
        for number in range(len(drained), until):
            transfer(0, 0, 0, 0, sent[number], twin, number, core).wait_send()
            drained.append(number)

    def arrive(band, k, first, length, core_of=core):
        transfer(band, band, k, first, length, twin, 0, core_of).wait_recv()

    kept, other = 2 * (y % 2), 2 - 2 * (y % 2)
    for half in (0, 2):
        send(0, 0, 0, half, 2, up, down)
    for half in (kept, other):
        send(0, 1, 0, half, 2, outer)
    send(0, 3, 0, 2 * zl, 2, beyond)
    send(0, 0, 0, 0, 4, twin)

    def search(_, span):
        low, high = span
        middle = (low + high) // 2
        first = segment[middle] == 0
        return jnp.where(first, middle + 1, low), jnp.where(first, high, middle)

    boundary, _ = lax.fori_loop(0, 12, search, (0, SLABS * ROWS - 1))
    my_slab = order[seq]

    loads[0].wait()
    loads[1].wait()
    row = lax.broadcasted_iota(jnp.int32, (ROWS, ROWS), 0)
    column = lax.broadcasted_iota(jnp.int32, (ROWS, ROWS), 1)
    one_hot = (row == column).astype(BF16)

    def absorb(j, _):
        two = queries[:, pl.ds(pl.multiple_of(j * 384, 384), 384)]
        for i in range(2):
            mine = two[:, i * 192 : i * 192 + 192]
            rows = pl.ds(pl.multiple_of((2 * j + i) * ROWS, ROWS), ROWS)
            wide_q[rows, :LATENT] = dot(mine[:, :NOPE], w_key[2 * j + i]).astype(BF16)
            wide_q[rows, LATENT:] = jnp.concatenate([mine[:, NOPE:], one_hot], axis=1)
        return 0

    lax.fori_loop(0, HEADS // 2, absorb, 0)

    query_pos = my_slab * ROWS + row
    first_live = jnp.where(query_pos >= boundary, boundary, 0)

    def cover(place, _):
        for band, zh_of in enumerate((zh, zh_outer, zh_inner, zh_far)):
            key_pos = order[slab((x + place // 2) % 4, zh_of, place % 2)] * ROWS + column
            live = (key_pos >= first_live) & (key_pos <= query_pos)
            bands[band][place, KEY:] = jnp.where(live, 0.0, NEGATIVE).astype(BF16)
        return 0

    lax.fori_loop(0, BAND, cover, 0)

    def own_near(k, onward, passed):
        arrive(0, k, 0, 2)
        arrive(0, k, 2, 2)
        send(0, 0, k, passed, 2, onward)
        send(0, 0, k, 0, 4, twin)

    def own_far():
        for half in (0, 2):
            arrive(0, 2, half, 2)
        send(0, 0, 2, 0, 4, twin)

    def next_door():
        arrive(1, 0, kept, 2)
        send(1, 1, 0, kept, 2, up, down)
        send(1, 2, 0, kept, 2, inner)
        arrive(1, 0, other, 2)
        send(1, 2, 0, other, 2, inner)
        send(1, 1, 0, 0, 4, twin)

    def one_further():
        arrive(2, 0, kept, 2)
        send(2, 2, 0, kept, 2, up, down)
        arrive(2, 0, other, 2)
        send(2, 2, 0, 0, 4, twin)

    def from_beyond():
        arrive(3, 0, 2 - 2 * zl, 2)
        send(3, 3, 0, 2 - 2 * zl, 2, inner)

    def far_whole():
        arrive(3, 0, 2 * zl, 2)
        send(3, 3, 0, kept, 2, up, down)
        send(3, 3, 0, 0, 4, twin)

    def near(band):
        for k, onward, part, side in ((3, up, 0, y_up), (1, down, 1, y_down)):
            arrive(band, k, kept, 2)
            send(band, band, k, kept + part, 1, onward)
            send(band, band, k, kept, 2, side, twin)

    def far(band):
        for part, side in ((0, y_up), (1, y_down)):
            arrive(band, 2, kept + part, 1)
            send(band, band, 2, kept + part, 1, side)
        send(band, band, 2, kept, 2, twin)

    def side_near(band):
        for k in (3, 1):
            arrive(band, k, other, 2)
            send(band, band, k, other, 2, twin)

    def side_far(band):
        for part in range(2):
            arrive(band, 2, other + part, 1)
        send(band, band, 2, other, 2, twin)

    def complete(group):
        for band, k in group:
            if band == 0 or k == 0:
                arrive(band, k, 0, 4, 1 - core)
            else:
                for half in (0, 2):
                    arrive(band, k, half, 2, 1 - core)

    groups = (
        ((0, 0), (0, 3), (0, 1), (1, 0)),
        ((0, 2), (2, 0), (1, 3), (1, 1)),
        ((3, 0), (1, 2), (2, 3), (2, 1)),
        ((3, 3), (3, 1), (2, 2), (3, 2)),
    )
    polls = (
        {1: [from_beyond], 3: [lambda: near(1)], 5: [one_further, own_far]},
        {
            0: [lambda: near(2)], 2: [lambda: side_far(1), lambda: near(3)],
            5: [lambda: far(2)], 6: [lambda: side_near(2)],
        },
        {
            0: [lambda: far(3), lambda: side_near(3)], 1: [lambda: side_far(2)],
            5: [lambda: side_far(3)],
        },
        {},
    )
    before_group = ([], [far_whole, lambda: far(1), lambda: side_near(1)], [], [])

    next_door()
    own_near(3, up, 0)
    own_near(1, down, 2)

    scale = (NOPE + ROPE) ** -0.5 * LOG2E
    scores, tops = (scores_0, scores_1), (tops_0, tops_1)
    parts = range(0, BAND * ROWS, CHUNK)

    def rows_of(step):
        return pl.ds(pl.multiple_of(step * PAIR, PAIR), PAIR)

    def score(group, q, first, slot, top):
        band, k = groups[group][first // CHUNK]
        keys = jnp.concatenate([bands[band][2 * k], bands[band][2 * k + 1]], axis=1)
        s = dot(q, keys)
        scores[slot][:, pl.ds(first, CHUNK)] = s
        for i in range(0, CHUNK, 128):
            part = s[:, i : i + 128]
            top = part if top is None else jnp.maximum(top, part)
        return top

    def attend(group, step, slot, ahead):
        here = rows_of(step)
        top = jnp.broadcast_to(jnp.max(tops[slot][...], axis=1, keepdims=True), (PAIR, 128)) * scale
        if group == 0:
            sums = jnp.zeros((PAIR, 128), F32)
        else:
            before = best[here, :]
            top = jnp.maximum(top, before)
            fade = jnp.exp2(before - top)
            sums = total[here, :] * fade
        gained, next_top = None, None
        for first in parts:
            if ahead:
                next_top = score(group, wide_q[rows_of(step + 1), :], first, 1 - slot, next_top)
            weights = []
            for i in range(0, CHUNK, 128):
                w = jnp.exp2(scores[slot][:, pl.ds(first + i, 128)] * scale - top)
                sums = sums + w
                weights.append(w.astype(BF16))
            more = dot(jnp.concatenate(weights, axis=1), value[pl.ds(first, CHUNK), :])
            gained = more if gained is None else gained + more
        if ahead:
            tops[1 - slot][...] = next_top
        if group > 0:
            gained = gained + context[here, :] * jnp.concatenate([fade] * 4, axis=1)
        if group < 3:
            best[here, :] = top
            total[here, :] = sums
            context[here, :] = gained
            return
        finished = (gained / jnp.sum(sums, axis=1, keepdims=True)).astype(BF16)
        for i in range(2):
            h = 2 * step + i
            attended[:, pl.ds(pl.multiple_of(h * VHEAD, VHEAD), VHEAD)] = dot(
                finished[i * ROWS : (i + 1) * ROWS], w_value[h]
            ).astype(BF16)
        for i in range(7):
            deliver(step, i).start()

    def columns_of(who, step):
        return pl.ds(pl.multiple_of(who * (HEADS * VHEAD) + step * PAIR, PAIR), PAIR)

    def deliver(step, i):
        mate = mates[i][1]
        return pltpu.make_async_remote_copy(
            src_ref=attended.at[pl.ds(pl.multiple_of(mate * 16, 16), 16), columns_of(0, step)],
            dst_ref=out.at[:, columns_of(head, step)],
            send_sem=out_send.at[i], recv_sem=out_recv.at[i],
            device_id=mates[i], device_id_type=MESH,
        )

    for group in range(4):
        for wait in before_group[group]:
            wait()
        complete(groups[group])
        if group == 3:
            loads[2].wait()

        for i, (band, k) in enumerate(groups[group]):
            for c in range(2):
                taken = bands[band][2 * k + c, :LATENT]
                value[pl.ds((2 * i + c) * ROWS, ROWS), :] = taken.T
        top = None
        for first in parts:
            top = score(group, wide_q[rows_of(0), :], first, 0, top)
        tops[0][...] = top

        def go(i, _, group=group):
            for slot in range(2):
                attend(group, 2 * i + slot, slot, True)
                for n in range(slot, STEPS - 2, 2):
                    if n in polls[group]:

                        @pl.when(i == n // 2)
                        def _(n=n):
                            for wait in polls[group][n]:
                                wait()

            return 0

        lax.fori_loop(0, STEPS // 2 - 1, go, 0)
        attend(group, STEPS - 2, 0, True)
        for wait in polls[group].get(STEPS - 2, []):
            wait()
        attend(group, STEPS - 1, 1, False)

    out[:, pl.ds(pl.multiple_of(head * (HEADS * VHEAD), 128), HEADS * VHEAD)] = attended[
        pl.ds(pl.multiple_of(head * 16, 16), 16), :
    ]
    drain(len(sent))
    for i in range(7):
        mate, sender = mates[i][1], (head + 7 - i) % 8
        whole = pltpu.make_async_remote_copy(
            src_ref=attended.at[pl.ds(pl.multiple_of(mate * 16, 16), 16), :],
            dst_ref=out.at[:, pl.ds(pl.multiple_of(sender * (HEADS * VHEAD), 128), HEADS * VHEAD)],
            send_sem=out_send.at[i], recv_sem=out_recv.at[i],
            device_id=mates[i], device_id_type=MESH,
        )
        whole.wait_send()
        whole.wait_recv()


def shards(queries, latent_keys, w_key_up, w_value_up, slab_order, segment_ids):
    rows = HEADS * ROWS
    return pl.pallas_call(
        kernel,
        out_shape=jax.ShapeDtypeStruct((16, 8 * HEADS * VHEAD), BF16),
        in_specs=[
            pl.BlockSpec(memory_space=pltpu.SMEM),
            pl.BlockSpec(memory_space=pltpu.SMEM),
            pl.BlockSpec(memory_space=pltpu.VMEM),
            pl.BlockSpec(memory_space=pl.ANY),
            pl.BlockSpec(memory_space=pl.ANY),
            pl.BlockSpec(memory_space=pl.ANY),
        ],
        out_specs=pl.BlockSpec(memory_space=pltpu.VMEM),
        scratch_shapes=[
            pltpu.VMEM((BAND, WIDE, ROWS), BF16),
            pltpu.VMEM((BAND, WIDE, ROWS), BF16),
            pltpu.VMEM((BAND, WIDE, ROWS), BF16),
            pltpu.VMEM((BAND, WIDE, ROWS), BF16),
            pltpu.VMEM((rows, WIDE), BF16),
            pltpu.VMEM((BAND * ROWS, LATENT), BF16),
            pltpu.VMEM((PAIR, BAND * ROWS), F32),
            pltpu.VMEM((PAIR, BAND * ROWS), F32),
            pltpu.VMEM((PAIR, 128), F32),
            pltpu.VMEM((PAIR, 128), F32),
            pltpu.VMEM((rows, 128), F32),
            pltpu.VMEM((rows, 128), F32),
            pltpu.VMEM((rows, LATENT), F32),
            pltpu.VMEM((ROWS, HEADS * VHEAD), BF16),
            pltpu.VMEM((ROWS, HEADS * (NOPE + ROPE)), BF16),
            pltpu.VMEM((HEADS, NOPE, LATENT), BF16),
            pltpu.VMEM((HEADS, LATENT, VHEAD), BF16),
            pltpu.SemaphoreType.DMA((3,)),
            pltpu.SemaphoreType.DMA((72,)),
            pltpu.SemaphoreType.DMA((4, BAND, 4)),
            pltpu.SemaphoreType.DMA((7,)),
            pltpu.SemaphoreType.DMA((7,)),
        ],
        compiler_params=pltpu.CompilerParams(
            collective_id=0, has_side_effects=True, vmem_limit_bytes=56 * 2**20
        ),
        cost_estimate=pl.CostEstimate(
            flops=20 * 10**9, bytes_accessed=6 * 2**20, transcendentals=8 * 10**6
        ),
    )(slab_order, segment_ids, latent_keys.T, queries, w_key_up, w_value_up)


def solution(mesh):
    in_specs = (
        P("seq", "head"),
        P("seq", None),
        P("head", None, None),
        P("head", None, None),
        P(),
        P(),
    )
    out_specs = P(("seq", "head"), None)
    return jax.shard_map(shards, mesh=mesh, in_specs=in_specs, out_specs=out_specs, check_vma=False)
```
